256 devices in a mesh: dp: 64 (over z, y, core), group: 4 (over x).
Axes of the slice: x: 4, y: 4, z: 8, core: 2. Of those that a mesh axis runs over, the one named last changes fastest.
Arguments:
- features: bfloat16 [256, 1536, 1024], P(('dp', 'group')), may hold values from -6 to 6
- targets: int32 [256, 4, 1536], P(('dp', 'group')), may hold values from 0 to 1024, as said below
- matches: int32 [256, 1536], P(('dp', 'group')), may hold values from -1 to 383, as said below
- queries: bfloat16 [24576, 768], P(('dp', 'group')), may hold values from -6 to 6
- class_weight: bfloat16 [1024, 768], replicated, may hold values from -0.1875 to 0.1875
- trunk_weight: bfloat16 [1024, 1024], replicated, may hold values from -0.1875 to 0.1875
- head_rows: bfloat16 [6, 1024], replicated
Outputs:
- loss: float32 [], replicated
- query_grad: float32 [24576, 768], P(('dp', 'group'))
- class_grad: float32 [1024, 768], P('dp')
- box_grad: float32 [4, 1024], replicated
- side_grad: float32 [2, 1024], replicated
The draws below stay inside these ranges and needn't reach their ends.
Inputs may be any that keep to these rules, and one draw needn't show every extreme that they name: `matches`: -1 marks a box matched to no query; any other value is the matched query's index among the 384 queries of the image's group; every image has 32 or more matched boxes. `targets`: the four rows are left, top, right, bottom in units of 1 / 1024 of the image side; right - left and bottom - top are 64 or more.
All inputs are finite; a program needn't handle non-finite values.
Results may differ from the reference program's by a relative error of at most 0.013.
Values may be sent and summed in bfloat16 or wider, within the bound.
A program may use at most 64 MiB of HBM per device.

```python
import jax
import jax.numpy as jnp
from jax import lax

E = 1024
D = 768
ROWS = 1536
GRID = 72
POS = 32
QUANT = 1024
IMAGES = 256
Q = 384
QTOT = 24576
N_GROUP = 4


def draw_matches(key, part):
    key = jax.random.fold_in(key, 11)

    def single(image):
        inner = jax.random.fold_in(key, image)
        order_key, pick_key, extra_key = jax.random.split(inner, 3)
        wanted = POS + 2 * POS * image // max(IMAGES - 1, 1) + jax.random.randint(extra_key, (), 0, POS // 2 + 1)
        order = jax.random.permutation(order_key, ROWS)
        ranking = jnp.zeros((ROWS,), jnp.int32).at[order].set(jnp.arange(ROWS, dtype=jnp.int32))
        picks = jax.random.randint(pick_key, (ROWS,), 0, Q)
        picks = jnp.where(ranking == 0, Q - 1, picks)
        return jnp.where(ranking < wanted, picks, -1)
    return jax.vmap(single)(jnp.arange(IMAGES, dtype=jnp.int32)).astype(jnp.int32)


def draw_targets(key, part):
    key = jax.random.fold_in(key, 23)
    width_key, height_key, across_key, down_key = jax.random.split(key, 4)
    shape = (IMAGES, ROWS)
    widths = jax.random.randint(width_key, shape, QUANT // 16, QUANT // 2 + 1)
    heights = jax.random.randint(height_key, shape, QUANT // 16, QUANT // 2 + 1)
    jitter_x = jax.random.randint(across_key, shape, -(QUANT // 16), QUANT // 16 + 1)
    jitter_y = jax.random.randint(down_key, shape, -(QUANT // 16), QUANT // 16 + 1)
    index = jnp.arange(ROWS, dtype=jnp.int32)[None, :]
    center_x = (index % GRID * 2 + 1) * QUANT // (2 * GRID)
    center_y = (index // GRID * 2 + 1) * QUANT // (2 * GRID)
    lefts = jnp.clip(center_x + jitter_x - widths // 2, 0, QUANT - widths)
    tops = jnp.clip(center_y + jitter_y - heights // 2, 0, QUANT - heights)
    lefts = jnp.where(index == 0, 0, jnp.where(index == 1, QUANT - widths, lefts))
    tops = jnp.where(index == 0, 0, jnp.where(index == 1, QUANT - heights, tops))
    return jnp.stack([lefts, tops, lefts + widths, tops + heights], 1).astype(jnp.int32)


def draw_head_rows(key, part):
    key = jax.random.fold_in(key, 37)
    noise = jax.random.normal(key, (6, E), jnp.float32)
    offset = jnp.array([0.0, 0.0, 11.0, 11.0, 0.0, 0.0], jnp.float32)[:, None] / E
    return (noise * E ** (-0.5) + offset).astype(jnp.bfloat16)


def shard_levels(stream_key, shape, shards, smallest, high):
    loudness, own = 1.0, jax.random.fold_in(stream_key, 6)
    for dim, blocks in shards:
        draws = jnp.exp(jax.random.uniform(jax.random.fold_in(own, dim), (blocks,), jnp.float32, smallest / len(shards), high / len(shards)))
        loudness = loudness * jnp.repeat(draws, shape[dim] // blocks).reshape([-1 if axis == dim else 1 for axis in range(len(shape))])
    return loudness


def bell_draw(own_key, extent, deviation, bound, shards=(), kind=jnp.bfloat16):
    loudness = shard_levels(own_key, extent, shards, -0.22, 0.18) if shards else 1.0
    entries = jax.random.normal(own_key, extent, jnp.float32) * deviation * loudness
    return jnp.minimum(jnp.maximum(entries, -bound), bound).astype(kind)


def setup_inputs(seed: int = 0) -> dict:
    key_of = jax.random.split(jax.random.key(seed), 8)
    features = bell_draw(key_of[0], (IMAGES, ROWS, E), 1.0, 6.0, ((0, 256),))
    targets = draw_targets(jax.random.fold_in(key_of[7], 71), 0)
    matches = draw_matches(jax.random.fold_in(key_of[7], 71), 0)
    queries = bell_draw(key_of[3], (QTOT, D), 1.0, 6.0, ((0, 256),))
    class_weight = bell_draw(key_of[4], (E, D), E ** -0.5, 0.1875)
    trunk_weight = bell_draw(key_of[5], (E, E), E ** -0.5, 0.1875)
    head_rows = draw_head_rows(jax.random.fold_in(key_of[7], 71), 0)
    return dict(features=features, targets=targets, matches=matches, queries=queries, class_weight=class_weight, trunk_weight=trunk_weight, head_rows=head_rows)


ALPHA = 0.25
GIOU_WEIGHT = 2.0
LOGIT_BIAS = -4.0
EPSILON = 1e-06

def contract(left, right, left_dim, right_dim):
    return lax.dot_general(left, right, (((left_dim,), (right_dim,)), ((), ())), preferred_element_type=jnp.float32)

def logit(value):
    return jnp.log(value) - jnp.log1p(-value)

def box_prior(length):
    index = jnp.arange(length, dtype=jnp.int32)
    column = (index % GRID).astype(jnp.float32)
    line = (index // GRID).astype(jnp.float32)
    across = logit((column + 0.5) / GRID)
    down = logit((line + 0.5) / GRID)
    size = logit(jnp.full((length,), 1.0 / GRID, jnp.float32))
    return jnp.stack([across, down, size, size], 0)

def box_loss(box_raw, corners, weight):
    box = jax.nn.sigmoid(box_raw)
    left = box[0] - 0.5 * box[2]
    right = box[0] + 0.5 * box[2]
    top = box[1] - 0.5 * box[3]
    bottom = box[1] + 0.5 * box[3]
    inter_w = jnp.maximum(jnp.minimum(right, corners[2]) - jnp.maximum(left, corners[0]), 0.0)
    inter_h = jnp.maximum(jnp.minimum(bottom, corners[3]) - jnp.maximum(top, corners[1]), 0.0)
    inter = inter_w * inter_h
    union = box[2] * box[3] + (corners[2] - corners[0]) * (corners[3] - corners[1]) - inter
    outer_w = jnp.maximum(right, corners[2]) - jnp.minimum(left, corners[0])
    outer_h = jnp.maximum(bottom, corners[3]) - jnp.minimum(top, corners[1])
    enclose = outer_w * outer_h
    giou = inter / union - (enclose - union) / enclose
    return jnp.sum(weight * (1.0 - giou))

def focal_parts(logits, is_match):
    prob = jax.nn.sigmoid(logits)
    log_pos = jax.nn.log_sigmoid(logits)
    log_neg = jax.nn.log_sigmoid(-logits)
    other = 1.0 - prob
    loss_pos = -ALPHA * other * other * log_pos
    loss_neg = -(1.0 - ALPHA) * prob * prob * log_neg
    grad_pos = ALPHA * other * other * (2.0 * prob * log_pos - other)
    grad_neg = (1.0 - ALPHA) * prob * prob * (prob - 2.0 * other * log_neg)
    total = jnp.sum(jnp.where(is_match, loss_pos, loss_neg))
    return (total, jnp.where(is_match, grad_pos, grad_neg))

def image_terms(features_one, corners_int, matches_one, group_queries, class_weight, trunk_weight, head_rows):
    length = features_one.shape[0]
    width = group_queries.shape[0]
    hidden = jax.nn.gelu(jnp.dot(features_one, trunk_weight, preferred_element_type=jnp.float32)).astype(jnp.bfloat16)
    embedding = jnp.dot(features_one, class_weight, preferred_element_type=jnp.float32)
    embed_norms = jnp.sqrt(lax.optimization_barrier(jnp.sum(embedding * embedding, axis=1, keepdims=True)) + EPSILON)
    exact_units = embedding / embed_norms
    units = exact_units.astype(jnp.bfloat16)
    box_raw = contract(head_rows[0:4], hidden, 1, 1) + box_prior(length)
    side = contract(head_rows[4:6], features_one, 1, 1)
    shift = side[0] + LOGIT_BIAS
    scale_pre = side[1]
    scale = jax.nn.elu(scale_pre) + 1.0
    cosine = contract(units, group_queries, 1, 1)
    logits = (cosine + shift[:, None]) * scale[:, None]
    is_match = matches_one[:, None] == jnp.arange(width, dtype=jnp.int32)[None, :]
    focal_sum, dlogits = focal_parts(logits, is_match)
    grad_logits = (dlogits * scale[:, None]).astype(jnp.bfloat16)
    d_shift = lax.optimization_barrier(jnp.sum(dlogits, axis=1))
    d_scale = lax.optimization_barrier(jnp.sum(dlogits * (cosine + shift[:, None]), axis=1))
    d_scale_pre = d_scale * jnp.where(scale_pre > 0, 1.0, jnp.exp(scale_pre))
    corners = corners_int.astype(jnp.float32) / QUANT
    weight = (matches_one >= 0).astype(jnp.float32)
    giou_sum, pullback = jax.vjp(lambda value: box_loss(value, corners, weight), box_raw)
    d_raw = GIOU_WEIGHT * pullback(jnp.ones_like(giou_sum))[0]
    row_grads = jnp.concatenate([d_raw, d_shift[None, :], d_scale_pre[None, :]], 0).astype(jnp.bfloat16)
    small_terms = jnp.concatenate([contract(row_grads[0:4], hidden, 1, 0), contract(row_grads[4:6], features_one, 1, 0)], 0)
    d_units = jnp.dot(grad_logits, group_queries, preferred_element_type=jnp.float32)
    d_embedding = ((d_units - exact_units * lax.optimization_barrier(jnp.sum(exact_units * d_units, axis=1, keepdims=True))) / embed_norms).astype(jnp.bfloat16)
    return (focal_sum, giou_sum, grad_logits, units, d_embedding, small_terms)

def reference(features, targets, matches, queries, class_weight, trunk_weight, head_rows):
    exact_in = queries.astype(jnp.float32)
    query_norms = jnp.sqrt(lax.optimization_barrier(jnp.sum(exact_in * exact_in, axis=1, keepdims=True)) + EPSILON)
    exact_queries = exact_in / query_norms
    unit_queries = exact_queries.astype(jnp.bfloat16)

    def visit(carry, item):
        class_sum, small_sum, focal_all, giou_all, count_all, query_sums = carry
        features_one, corners_one, matches_one, image = item
        start = image // N_GROUP * Q
        group_queries = lax.dynamic_slice_in_dim(unit_queries, start, Q, 0)
        focal_sum, giou_sum, grad_logits, units, d_embedding, small_terms = image_terms(features_one, corners_one, matches_one, group_queries, class_weight, trunk_weight, head_rows)
        class_sum = class_sum + contract(features_one, d_embedding, 0, 0)
        block = lax.dynamic_slice_in_dim(query_sums, start, Q, 0) + contract(grad_logits, units, 0, 0)
        query_sums = lax.dynamic_update_slice_in_dim(query_sums, block, start, 0)
        count_one = jnp.sum((matches_one >= 0).astype(jnp.float32))
        return ((class_sum, small_sum + small_terms, focal_all + focal_sum, giou_all + giou_sum, count_all + count_one, query_sums), None)
    start_carry = (jnp.zeros((E, D), jnp.float32), jnp.zeros((6, E), jnp.float32), jnp.zeros((), jnp.float32), jnp.zeros((), jnp.float32), jnp.zeros((), jnp.float32), jnp.zeros((QTOT, D), jnp.float32))
    items = (features, targets, matches, jnp.arange(IMAGES, dtype=jnp.int32))
    final, _ = lax.scan(visit, start_carry, items)
    class_sum, small_sum, focal_all, giou_all, positives, query_sums = final
    loss = (focal_all + GIOU_WEIGHT * giou_all) / positives
    query_grad = (query_sums - exact_queries * lax.optimization_barrier(jnp.sum(exact_queries * query_sums, axis=1, keepdims=True))) / query_norms / positives
    return (loss, query_grad, class_sum / positives, small_sum[0:4] / positives, small_sum[4:6] / positives)
```

```python
import functools

import jax
import jax.numpy as jnp
import numpy as np
from jax import lax
from jax.experimental import pallas as pl
from jax.experimental.pallas import tpu as pltpu
from jax.sharding import PartitionSpec as P

MESH = pl.DeviceIdType.MESH
F32 = jnp.float32
BF16 = jnp.bfloat16

GRID = 72
QUANT = 1024
ALPHA = 0.25
GIOU_WEIGHT = 2.0
LOGIT_BIAS = -4.0
EPSILON = 1e-06

NX, NY, NZ, NC = 4, 4, 8, 2
E, D, ROWS, Q = 1024, 768, 1536, 384
QROWS = Q // NX
SHARE = E // (NZ * NY * NC)
HALF = D // 2
BLOCK = 256
PEERS = 1 + (NX - 1) + (NY - 1) + (NZ - 1)


def contract(left, right, left_dim, right_dim):
    return lax.dot_general(
        left, right, (((left_dim,), (right_dim,)), ((), ())), preferred_element_type=F32
    )


def box_prior(length):
    index = np.arange(length)

    def logit(value):
        return np.log(value) - np.log1p(-value)

    across = logit((index % GRID + 0.5) / GRID)
    down = logit((index // GRID + 0.5) / GRID)
    size = np.full((length,), logit(1.0 / GRID))
    return np.stack([across, down, size, size], 0).astype(np.float32)


def box_loss(box_raw, corners, weight):
    box = jax.nn.sigmoid(box_raw)
    cx, cy, bw, bh = (box[i : i + 1] for i in range(4))
    c0, c1, c2, c3 = (corners[i : i + 1] for i in range(4))
    left = cx - 0.5 * bw
    right = cx + 0.5 * bw
    top = cy - 0.5 * bh
    bottom = cy + 0.5 * bh
    inter_w = jnp.maximum(jnp.minimum(right, c2) - jnp.maximum(left, c0), 0.0)
    inter_h = jnp.maximum(jnp.minimum(bottom, c3) - jnp.maximum(top, c1), 0.0)
    inter = inter_w * inter_h
    union = bw * bh + (c2 - c0) * (c3 - c1) - inter
    outer_w = jnp.maximum(right, c2) - jnp.minimum(left, c0)
    outer_h = jnp.maximum(bottom, c3) - jnp.minimum(top, c1)
    enclose = outer_w * outer_h
    giou = inter / union - (enclose - union) / enclose
    return weight * (1.0 - giou)


def gelu(value):
    inner = value * (0.7978845608028654 + 0.035677408136300125 * (value * value))
    half = 0.5 * value
    return half + half * jnp.tanh(inner)


def rows_of(index, size):
    return pl.ds(pl.multiple_of(index * size, size), size)


def kernel(
    queries_hbm, features_hbm, cw_hbm, tw_hbm, targets_ref, matches_ref, heads_ref, prior_ref,
    loss_out, query_out, class_out, box_out, side_out,
    feat, feat_t, cw, tw, own_q, all_q, unit_q, exact, inv_norm, units, hidden, raw, side,
    cosine, grads, d_rows, d_emb, small, small_p, small_two, small_z, small_v, small_y, small_vy,
    small_x, small_vx, small_all, q_send, q_recv, g_both, g_recv, s0, s1, r1y, r1x, y2, x2,
    r2x, r2y, t3, r3, fin,
    load_sem, q_ssem, q_rsem, sp_sem, sz_ssem, sz_rsem, sy_ssem, sy_rsem, sx_ssem, sx_rsem,
    sa_ssem, sa_rsem, qs_ssem, qs_rsem, gp_ssem, gp_rsem, y1_ssem, y1_rsem, x1_ssem, x1_rsem,
    x2_ssem, x2_rsem, y2_ssem, y2_rsem, z3_ssem, z3_rsem, f_ssem, f_rsem,
):
    dp = lax.axis_index("dp")
    x = lax.axis_index("group")
    core = dp % NC
    y = (dp // NC) % NY
    z = dp // (NC * NY)

    def at(zz, yy, cc, xx):
        return ((zz * NY + yy) * NC + cc, xx)

    pair = at(z, y, 1 - core, x)
    x_peer = lambda d: at(z, y, core, (x + d) % NX)
    y_peer = lambda d: at(z, (y + d) % NY, core, x)
    z_peer = lambda d: at((z + d) % NZ, y, core, x)
    xs, ys, zs = range(1, NX), range(1, NY), range(1, NZ)

    def remote(src, dst, ssem, rsem, device):
        return pltpu.make_async_remote_copy(
            src_ref=src, dst_ref=dst, send_sem=ssem, recv_sem=rsem,
            device_id=device, device_id_type=MESH,
        )

    loads = [
        pltpu.make_async_copy(queries_hbm, own_q, load_sem.at[0]),
        pltpu.make_async_copy(features_hbm.at[0], feat, load_sem.at[1]),
        pltpu.make_async_copy(cw_hbm, cw, load_sem.at[2]),
        pltpu.make_async_copy(tw_hbm, tw, load_sem.at[3]),
    ]
    for load in loads:
        load.start()

    barrier = pltpu.get_barrier_semaphore()
    peers = [pair] + [x_peer(d) for d in xs] + [y_peer(d) for d in ys] + [z_peer(d) for d in zs]
    for peer in peers:
        pl.semaphore_signal(barrier, inc=1, device_id=peer, device_id_type=MESH)
    loads[0].wait()
    all_q[x] = own_q[...]
    pl.semaphore_wait(barrier, PEERS)

    q_copies = [
        remote(own_q, all_q.at[x], q_ssem.at[d - 1], q_rsem.at[d - 1], x_peer(d)) for d in xs
    ]
    for copy in q_copies:
        copy.start()

    loads[1].wait()
    loads[2].wait()

    def embed(i, carry):
        rows = rows_of(i, BLOCK)
        emb = contract(feat[rows, :], cw[...], 1, 0)
        inv = lax.rsqrt(jnp.sum(emb * emb, axis=1, keepdims=True) + EPSILON)
        unit = emb * inv
        exact[rows, :] = unit
        units[rows, :] = unit.astype(BF16)
        inv_norm[rows, :] = inv
        return carry

    lax.fori_loop(0, ROWS // BLOCK, embed, 0)
    loads[3].wait()

    def box_hidden(i, carry):
        rows = rows_of(i, BLOCK)
        block = feat[rows, :]
        hid = gelu(contract(block, tw[...], 1, 0)).astype(BF16)
        hidden[rows, :] = hid
        raw[:, rows] = contract(heads_ref[...], hid, 1, 1)
        side[:, rows] = contract(heads_ref[...], block, 1, 1)
        feat_t[:, rows] = block.T
        return carry

    lax.fori_loop(0, ROWS // BLOCK, box_hidden, 0)

    matches = matches_ref[...]
    weight = (matches >= 0).astype(F32)
    corners = targets_ref[0].astype(F32) * (1.0 / QUANT)
    terms, pullback = jax.vjp(
        lambda value: box_loss(value, corners, weight), raw[0:4, :] + prior_ref[...]
    )
    d_raw = (GIOU_WEIGHT * pullback(jnp.ones_like(terms))[0]).astype(BF16)
    small[0:4, :] = contract(d_raw, hidden[...], 1, 0)

    for copy in q_copies:
        copy.wait()
    for g in range(NX):
        rows = all_q[g].astype(F32)
        inv = lax.rsqrt(jnp.sum(rows * rows, axis=1, keepdims=True) + EPSILON)
        unit_q[g * QROWS : (g + 1) * QROWS, :] = (rows * inv).astype(BF16)

    step = 32

    def focal(i, loss_sum):
        cols = rows_of(i, BLOCK)
        cosine[...] = contract(unit_q[...], units[cols, :], 1, 1)
        shift = side[4:5, cols] + LOGIT_BIAS
        pre = side[5:6, cols]
        decay = jnp.exp(jnp.minimum(pre, 0.0))
        scale = jnp.where(pre > 0, pre + 1.0, decay)
        match = matches_ref[:, cols]

        def block(j, carry):
            loss, d_shift, d_scale = carry
            rows = rows_of(j, step)
            base = cosine[rows, :] + shift
            index = lax.broadcasted_iota(jnp.int32, (step, BLOCK), 0)
            hit = index == match - j * step
            logit = base * scale
            value = jnp.where(hit, -logit, logit)
            factor = jnp.where(hit, -ALPHA, 1.0 - ALPHA)
            small_exp = jnp.exp(-jnp.abs(value))
            log_one = jnp.log1p(small_exp)
            big = jnp.exp(-log_one)
            little = small_exp * big
            positive = value >= 0
            prob = jnp.where(positive, big, little)
            other = jnp.where(positive, little, big)
            neg_log = jnp.maximum(value, 0.0) + log_one
            square = factor * (prob * prob)
            loss = loss + (jnp.abs(square) * neg_log).reshape(step // 8, 8, BLOCK).sum(0)
            other_log = other * neg_log
            d_logit = square * (prob + (other_log + other_log))
            d_shift = d_shift + d_logit.reshape(step // 8, 8, BLOCK).sum(0)
            d_scale = d_scale + (d_logit * base).reshape(step // 8, 8, BLOCK).sum(0)
            grads[rows, cols] = (d_logit * scale).astype(BF16)
            return loss, d_shift, d_scale

        zero = jnp.zeros((8, BLOCK), F32)
        loss, d_shift, d_scale = lax.fori_loop(0, Q // step, block, (loss_sum, zero, zero))
        d_rows[0:1, cols] = jnp.sum(d_shift, axis=0, keepdims=True)
        d_rows[1:2, cols] = jnp.sum(d_scale, axis=0, keepdims=True) * jnp.where(
            pre > 0, 1.0, decay
        )
        return loss

    focal_sum = lax.fori_loop(0, ROWS // BLOCK, focal, jnp.zeros((8, BLOCK), F32))

    small[4:6, :] = contract(d_rows[...].astype(BF16), feat[...], 1, 0)
    fold = lambda row: row[:, 0:512] + row[:, 512:1024] + row[:, 1024:1536]
    focal_row = jnp.sum(focal_sum, axis=0, keepdims=True)
    small[6:7, 0:512] = GIOU_WEIGHT * fold(terms)
    small[6:7, 0:BLOCK] += focal_row
    small[6:7, 512:1024] = fold(weight)
    small[7:8, :] = jnp.zeros((1, E), F32)
    small_pair = remote(small, small_p, sp_sem.at[0], sp_sem.at[1], pair)
    small_pair.start()

    for n in range(D // BLOCK):
        cols = slice(n * BLOCK, (n + 1) * BLOCK)
        part = contract(grads[...], units[:, cols], 1, 0).astype(BF16)
        for g in range(NX):
            q_send[g, :, cols] = part[g * QROWS : (g + 1) * QROWS, :]
    qs_copies = [
        remote(q_send.at[(x + d) % NX], q_recv.at[d - 1], qs_ssem.at[d - 1], qs_rsem.at[d - 1], x_peer(d))
        for d in xs
    ]
    for copy in qs_copies:
        copy.start()

    small_pair.wait()
    for k in range(NZ):
        lanes = slice(k * 128, (k + 1) * 128)
        small_two[k] = small[:, lanes] + small_p[:, lanes]
    sz_copies = [
        remote(small_two.at[(z + d) % NZ], small_z.at[d - 1], sz_ssem.at[d - 1], sz_rsem.at[d - 1], z_peer(d))
        for d in zs
    ]
    for copy in sz_copies:
        copy.start()

    def embedding_grad(i, carry):
        rows = rows_of(i, BLOCK)
        d_units = contract(grads[:, rows], unit_q[...], 0, 0)
        unit = exact[rows, :]
        along = jnp.sum(unit * d_units, axis=1, keepdims=True)
        d_emb[rows, :] = ((d_units - unit * along) * inv_norm[rows, :]).astype(BF16)
        return carry

    lax.fori_loop(0, ROWS // BLOCK, embedding_grad, 0)

    for copy in sz_copies:
        copy.wait()
    small_v[...] = (
        ((small_two[z] + small_z[0]) + (small_z[1] + small_z[2]))
        + ((small_z[3] + small_z[4]) + (small_z[5] + small_z[6]))
    )
    sy_copies = [
        remote(small_v, small_y.at[d - 1], sy_ssem.at[d - 1], sy_rsem.at[d - 1], y_peer(d)) for d in ys
    ]
    for copy in sy_copies:
        copy.start()

    def pair_copy(j):
        return remote(g_both.at[1 - core, j], g_recv.at[j], gp_ssem.at[j], gp_rsem.at[j], pair)

    def y1_copy(k, j, d):
        return remote(s0.at[(y + d) % NY, k], r1y.at[d - 1, j], y1_ssem.at[d - 1, j], y1_rsem.at[d - 1, j], y_peer(d))

    def x1_copy(d):
        return remote(s1.at[(x + d) % NX], r1x.at[d - 1], x1_ssem.at[d - 1], x1_rsem.at[d - 1], x_peer(d))

    def chunk_of(j):
        return (x + 1 + j) % NX

    def produce(j):
        k = chunk_of(j)
        left = jnp.concatenate(
            [feat_t[rows_of(k, 128), :], feat_t[rows_of(k + NX, 128), :]], axis=0
        )
        for n in range(D // BLOCK):
            cols = slice(n * BLOCK, (n + 1) * BLOCK)
            part = contract(left, d_emb[:, cols], 1, 0).astype(BF16)
            part = part.reshape(2, NY, NC, SHARE, BLOCK)
            for cc in range(NC):
                g_both[cc, j, :, :, :, cols] = part[:, :, cc]

        pair_copy(j).start()

    def consume(j):
        k = chunk_of(j)
        pair_copy(j).wait()
        for h in range(2):
            both = (g_both[core, j, h].astype(F32) + g_recv[j, h].astype(F32)).astype(BF16)
            for yy in range(NY):
                s0[yy, k, h] = both[yy, :, 0:HALF]
                s1[k, yy, h] = both[yy, :, HALF:D]
        for d in ys:
            y1_copy(k, j, d).start()
        if j < NX - 1:
            x1_copy(j + 1).start()

    for j in range(NX):
        produce(j)
        if j > 0:
            consume(j - 1)
        if j == 1:
            for copy in sy_copies:
                copy.wait()
            small_vy[...] = (small_v[...] + small_y[1]) + (small_y[0] + small_y[2])
            sx_copies = [
                remote(small_vy, small_x.at[d - 1], sx_ssem.at[d - 1], sx_rsem.at[d - 1], x_peer(d))
                for d in xs
            ]
            for copy in sx_copies:
                copy.start()
        if j == 3:
            for copy in sx_copies:
                copy.wait()
            small_vx[...] = (small_vy[...] + small_x[1]) + (small_x[0] + small_x[2])
            small_all[z] = small_vx[...]
            sa_copies = [
                remote(small_vx, small_all.at[z], sa_ssem.at[d - 1], sa_rsem.at[d - 1], z_peer(d))
                for d in zs
            ]
            for copy in sa_copies:
                copy.start()
    consume(NX - 1)

    for d in xs:
        x1_copy(d).wait()
    for h in range(2):
        for yy in range(NY):
            total = s1[x, yy, h].astype(F32)
            for d in xs:
                total = total + r1x[d - 1, yy, h].astype(F32)
            x2[yy, h] = total.astype(BF16)
    y2_copies = [
        remote(x2.at[(y + d) % NY], r2y.at[d - 1], y2_ssem.at[d - 1], y2_rsem.at[d - 1], y_peer(d)) for d in ys
    ]
    for copy in y2_copies:
        copy.start()
    x2_copies = []
    for j in range(NX):
        k = chunk_of(j)
        for d in ys:
            y1_copy(k, j, d).wait()
        total = s0[y, k].astype(F32)
        for d in ys:
            total = total + r1y[d - 1, j].astype(F32)
        y2[j] = total.astype(BF16)
        if j < NX - 1:
            copy = remote(y2.at[j], r2x.at[j], x2_ssem.at[j], x2_rsem.at[j], x_peer(j + 1))
            copy.start()
            x2_copies.append(copy)

    for copy in y2_copies:
        copy.wait()
    total = x2[y].astype(F32)
    for d in ys:
        total = total + r2y[d - 1].astype(F32)
    t3[:, 1] = total.astype(BF16)
    for copy in x2_copies:
        copy.wait()
    total = y2[NX - 1].astype(F32)
    for d in xs:
        total = total + r2x[d - 1].astype(F32)
    t3[:, 0] = total.astype(BF16)

    def z3_copy(h):
        distance = (x + NX * h - z + NZ) % NZ
        slot = jnp.maximum(distance - 1, 0)
        return distance, remote(
            t3.at[h], r3.at[slot], z3_ssem.at[h], z3_rsem.at[slot], z_peer(distance)
        )

    for h in range(2):
        distance, copy = z3_copy(h)
        pl.when(distance != 0)(copy.start)

    for copy in sa_copies:
        copy.wait()
    for k in range(NZ):
        small[:, k * 128 : (k + 1) * 128] = small_all[k]
    per = 1.0 / jnp.sum(small[6:7, 512:1024], axis=1, keepdims=True)
    box_out[...] = small[0:4, :] * per
    side_out[...] = small[4:6, :] * per
    loss_out[...] = jnp.sum(small[6:7, 0:512], axis=1, keepdims=True) * per

    for copy in qs_copies:
        copy.wait()
    sums = q_send[x].astype(F32)
    for d in xs:
        sums = sums + q_recv[d - 1].astype(F32)
    mine = own_q[...].astype(F32)
    inv = lax.rsqrt(jnp.sum(mine * mine, axis=1, keepdims=True) + EPSILON)
    mine = mine * inv
    along = jnp.sum(mine * sums, axis=1, keepdims=True)
    query_out[...] = (sums - mine * along) * (inv * per)

    owner = x == z % NX
    f_copies = [remote(fin, fin, f_ssem.at[d - 1], f_rsem.at[0], x_peer(d)) for d in xs]

    @pl.when(owner)
    def _():
        total = t3[z // NX].astype(F32)
        for d in zs:
            remote(t3.at[0], r3.at[d - 1], z3_ssem.at[0], z3_rsem.at[d - 1], z_peer(d)).wait_recv()
            total = total + r3[d - 1].astype(F32)
        fin[...] = total
        for copy in f_copies:
            copy.start()
        for copy in f_copies:
            copy.wait_send()

    @pl.when(jnp.logical_not(owner))
    def _():
        f_copies[0].wait_recv()

    for h in range(2):
        distance, copy = z3_copy(h)
        pl.when(distance != 0)(copy.wait_send)
    class_out[:, 0:HALF] = fin[0] * per
    class_out[:, HALF:D] = fin[1] * per


def on_device(features, targets, matches, queries, class_weight, trunk_weight, head_rows):
    hbm = pl.BlockSpec(memory_space=pl.ANY)
    vmem = pl.BlockSpec(memory_space=pltpu.VMEM)
    dma = lambda *shape: pltpu.SemaphoreType.DMA(shape)
    buf = lambda kind, *shape: pltpu.VMEM(shape, kind)
    loss, query, classes, box, side = pl.pallas_call(
        kernel,
        out_shape=(
            jax.ShapeDtypeStruct((1, 1), F32),
            jax.ShapeDtypeStruct((QROWS, D), F32),
            jax.ShapeDtypeStruct((SHARE, D), F32),
            jax.ShapeDtypeStruct((4, E), F32),
            jax.ShapeDtypeStruct((2, E), F32),
        ),
        in_specs=[hbm] * 4 + [vmem] * 4,
        out_specs=[vmem] * 5,
        scratch_shapes=[
            buf(BF16, ROWS, E),
            buf(BF16, E, ROWS),
            buf(BF16, E, D),
            buf(BF16, E, E),
            buf(BF16, QROWS, D),
            buf(BF16, NX, QROWS, D),
            buf(BF16, Q, D),
            buf(F32, ROWS, D),
            buf(F32, ROWS, 1),
            buf(BF16, ROWS, D),
            buf(BF16, ROWS, E),
            buf(F32, 6, ROWS),
            buf(F32, 6, ROWS),
            buf(F32, Q, BLOCK),
            buf(BF16, Q, ROWS),
            buf(F32, 2, ROWS),
            buf(BF16, ROWS, D),
            buf(F32, 8, E),
            buf(F32, 8, E),
            buf(F32, NZ, 8, 128),
            buf(F32, NZ - 1, 8, 128),
            buf(F32, 8, 128),
            buf(F32, NY - 1, 8, 128),
            buf(F32, 8, 128),
            buf(F32, NX - 1, 8, 128),
            buf(F32, 8, 128),
            buf(F32, NZ, 8, 128),
            buf(BF16, NX, QROWS, D),
            buf(BF16, NX - 1, QROWS, D),
            buf(BF16, NC, NX, 2, NY, SHARE, D),
            buf(BF16, NX, 2, NY, SHARE, D),
            buf(BF16, NY, NX, 2, SHARE, HALF),
            buf(BF16, NX, NY, 2, SHARE, HALF),
            buf(BF16, NY - 1, NX, 2, SHARE, HALF),
            buf(BF16, NX - 1, NY, 2, SHARE, HALF),
            buf(BF16, NX, 2, SHARE, HALF),
            buf(BF16, NY, 2, SHARE, HALF),
            buf(BF16, NX - 1, 2, SHARE, HALF),
            buf(BF16, NY - 1, 2, SHARE, HALF),
            buf(BF16, 2, 2, SHARE, HALF),
            buf(BF16, NZ - 1, 2, SHARE, HALF),
            buf(F32, 2, SHARE, HALF),
            dma(4), dma(NX - 1), dma(NX - 1), dma(2),
            dma(NZ - 1), dma(NZ - 1), dma(NY - 1), dma(NY - 1), dma(NX - 1), dma(NX - 1),
            dma(NZ - 1), dma(NZ - 1), dma(NX - 1), dma(NX - 1), dma(NX), dma(NX),
            dma(NY - 1, NX), dma(NY - 1, NX), dma(NX - 1), dma(NX - 1),
            dma(NX - 1), dma(NX - 1), dma(NY - 1), dma(NY - 1),
            dma(2), dma(NZ - 1), dma(NX - 1), dma(1),
        ],
        compiler_params=pltpu.CompilerParams(
            collective_id=0, has_side_effects=True, vmem_limit_bytes=56 * 1024 * 1024
        ),
        cost_estimate=pl.CostEstimate(
            flops=11_000_000_000, bytes_accessed=8_000_000, transcendentals=4_000_000
        ),
    )(
        queries, features, class_weight, trunk_weight, targets, matches, head_rows,
        jnp.asarray(box_prior(ROWS)),
    )
    return loss[0, 0], query, classes, box, side


def solution(mesh):
    in_specs = (
        P(("dp", "group"), None, None),
        P(("dp", "group"), None, None),
        P(("dp", "group"), None),
        P(("dp", "group"), None),
        P(),
        P(),
        P(),
    )
    out_specs = (P(), P(("dp", "group"), None), P("dp", None), P(), P())
    return jax.shard_map(
        on_device, mesh=mesh, in_specs=in_specs, out_specs=out_specs, check_vma=False
    )
```

```python
import functools

import jax
import jax.numpy as jnp
import numpy as np
from jax import lax
from jax.experimental import pallas as pl
from jax.experimental.pallas import tpu as pltpu
from jax.sharding import PartitionSpec as P

MESH = pl.DeviceIdType.MESH
F32 = jnp.float32
BF16 = jnp.bfloat16

GRID = 72
QUANT = 1024
ALPHA = 0.25
GIOU_WEIGHT = 2.0
LOGIT_BIAS = -4.0
EPSILON = 1e-06

NX, NY, NZ, NC = 4, 4, 8, 2
E, D, ROWS, Q = 1024, 768, 1536, 384
QROWS = Q // NX
SHARE = E // (NZ * NY * NC)
HALF = D // 2
BLOCK = 768
TILE = 256
PEERS = 1 + (NX * NY - 1) + (NZ - 1)


def contract(left, right, left_dim, right_dim):
    return lax.dot_general(
        left, right, (((left_dim,), (right_dim,)), ((), ())), preferred_element_type=F32
    )


def box_prior(length):
    index = np.arange(length)

    def logit(value):
        return np.log(value) - np.log1p(-value)

    across = logit((index % GRID + 0.5) / GRID)
    down = logit((index // GRID + 0.5) / GRID)
    size = np.full((length,), logit(1.0 / GRID))
    return np.stack([across, down, size, size], 0).astype(np.float32)


def box_loss(box_raw, corners, weight):
    box = jax.nn.sigmoid(box_raw)
    cx, cy, bw, bh = (box[i : i + 1] for i in range(4))
    c0, c1, c2, c3 = (corners[i : i + 1] for i in range(4))
    left = cx - 0.5 * bw
    right = cx + 0.5 * bw
    top = cy - 0.5 * bh
    bottom = cy + 0.5 * bh
    inter_w = jnp.maximum(jnp.minimum(right, c2) - jnp.maximum(left, c0), 0.0)
    inter_h = jnp.maximum(jnp.minimum(bottom, c3) - jnp.maximum(top, c1), 0.0)
    inter = inter_w * inter_h
    union = bw * bh + (c2 - c0) * (c3 - c1) - inter
    outer_w = jnp.maximum(right, c2) - jnp.minimum(left, c0)
    outer_h = jnp.maximum(bottom, c3) - jnp.minimum(top, c1)
    enclose = outer_w * outer_h
    giou = inter / union - (enclose - union) / enclose
    return weight * (1.0 - giou)


def gelu(value):
    inner = value * (0.7978845608028654 + 0.035677408136300125 * (value * value))
    half = 0.5 * value
    return half + half * jnp.tanh(inner)


def rows_of(index, size):
    return pl.ds(pl.multiple_of(index * size, size), size)


def kernel(
    queries_hbm, features_hbm, cw_hbm, tw_hbm, targets_ref, matches_ref, heads_ref, prior_ref,
    loss_out, query_out, class_out, box_out, side_out,
    feat, cw, tw, own_q, all_q, unit_q, exact, inv_norm, units, hidden, raw, side,
    cosine, grads, d_rows, d_emb, small, small_p, small_two, small_z, small_v, small_xy, small_sum,
    small_all, q_send, q_recv, g_both, g_recv, s0, s1, r1y, r1x, t0, t1, r2a, r2b, u0, u1, r3a, r3b,
    load_sem, q_ssem, q_rsem, sp_sem, sz_ssem, sz_rsem, sxy_ssem, sxy_rsem,
    sa_ssem, sa_rsem, qs_ssem, qs_rsem, gp_ssem, gp_rsem, y1_ssem, y1_rsem, x1_ssem, x1_rsem,
    z0_ssem, z0_rsem, z1_ssem, z1_rsem, f0_ssem, f0_rsem, f1_ssem, f1_rsem,
):
    dp = lax.axis_index("dp")
    x = lax.axis_index("group")
    core = dp % NC
    y = (dp // NC) % NY
    z = dp // (NC * NY)

    def at(zz, yy, cc, xx):
        return ((zz * NY + yy) * NC + cc, xx)

    pair = at(z, y, 1 - core, x)
    x_peer = lambda d: at(z, y, core, (x + d) % NX)
    y_peer = lambda d: at(z, (y + d) % NY, core, x)
    xy_peer = lambda dy, dx: at(z, (y + dy) % NY, core, (x + dx) % NX)
    z_peer = lambda d: at((z + d) % NZ, y, core, x)
    xs, ys, zs = range(1, NX), range(1, NY), range(1, NZ)
    plane = [(dy, dx) for dy in range(NY) for dx in range(NX) if dy or dx]

    def remote(src, dst, ssem, rsem, device):
        return pltpu.make_async_remote_copy(
            src_ref=src, dst_ref=dst, send_sem=ssem, recv_sem=rsem,
            device_id=device, device_id_type=MESH,
        )

    loads = [
        pltpu.make_async_copy(queries_hbm, own_q, load_sem.at[0]),
        pltpu.make_async_copy(features_hbm.at[0], feat, load_sem.at[1]),
        pltpu.make_async_copy(cw_hbm, cw, load_sem.at[2]),
        pltpu.make_async_copy(tw_hbm, tw, load_sem.at[3]),
    ]
    for load in loads:
        load.start()

    barrier = pltpu.get_barrier_semaphore()
    peers = [pair] + [xy_peer(dy, dx) for dy, dx in plane] + [z_peer(d) for d in zs]
    for peer in peers:
        pl.semaphore_signal(barrier, inc=1, device_id=peer, device_id_type=MESH)
    loads[0].wait()
    all_q[x] = own_q[...]
    loads[1].wait()
    loads[2].wait()

    def embed(i, carry):
        rows = rows_of(i, BLOCK)
        emb = contract(feat[rows, :], cw[...], 1, 0)
        inv = lax.rsqrt(jnp.sum(emb * emb, axis=1, keepdims=True) + EPSILON)
        unit = emb * inv
        exact[rows, :] = unit
        units[rows, :] = unit.astype(BF16)
        inv_norm[rows, :] = inv
        return carry

    embed(0, 0)

    pl.semaphore_wait(barrier, PEERS)
    q_copies = [
        remote(own_q, all_q.at[x], q_ssem.at[d - 1], q_rsem.at[d - 1], x_peer(d)) for d in (1, 3, 2)
    ]
    for copy in q_copies:
        copy.start()
    embed(1, 0)
    loads[3].wait()

    def box_hidden(i, carry):
        rows = rows_of(i, BLOCK)
        block = feat[rows, :]
        hid = gelu(contract(block, tw[...], 1, 0)).astype(BF16)
        hidden[rows, :] = hid
        raw[:, rows] = contract(hid, heads_ref[...], 1, 1).T
        side[:, rows] = contract(block, heads_ref[...], 1, 1).T
        return carry

    lax.fori_loop(0, ROWS // BLOCK, box_hidden, 0)

    matches = matches_ref[...]
    weight = (matches >= 0).astype(F32)
    corners = targets_ref[0].astype(F32) * (1.0 / QUANT)
    terms, pullback = jax.vjp(
        lambda value: box_loss(value, corners, weight), raw[0:4, :] + prior_ref[...]
    )
    d_raw = (GIOU_WEIGHT * pullback(jnp.ones_like(terms))[0]).astype(BF16)
    small[0:4, :] = contract(d_raw, hidden[...], 1, 0)

    for copy in q_copies:
        copy.wait()
    for g in range(NX):
        rows = all_q[g].astype(F32)
        inv = lax.rsqrt(jnp.sum(rows * rows, axis=1, keepdims=True) + EPSILON)
        unit_q[g * QROWS : (g + 1) * QROWS, :] = (rows * inv).astype(BF16)

    step = 32

    def focal(i, loss_sum):
        cosine[...] = contract(unit_q[...], units[rows_of(i, BLOCK), :], 1, 1)

        def tile(n, loss_sum):
            cols = rows_of(i * (BLOCK // TILE) + n, TILE)
            here = rows_of(n, TILE)
            shift = side[4:5, cols] + LOGIT_BIAS
            pre = side[5:6, cols]
            decay = jnp.exp(jnp.minimum(pre, 0.0))
            scale = jnp.where(pre > 0, pre + 1.0, decay)
            match = matches_ref[:, cols]

            def block(j, carry):
                loss, d_shift, d_scale = carry
                rows = rows_of(j, step)
                base = cosine[rows, here] + shift
                index = lax.broadcasted_iota(jnp.int32, (step, TILE), 0)
                hit = index == match - j * step
                logit = base * scale
                value = jnp.where(hit, -logit, logit)
                factor = jnp.where(hit, -ALPHA, 1.0 - ALPHA)
                small_exp = jnp.exp(-jnp.abs(value))
                log_one = jnp.log1p(small_exp)
                big = jnp.exp(-log_one)
                little = small_exp * big
                positive = value >= 0
                prob = jnp.where(positive, big, little)
                other = jnp.where(positive, little, big)
                neg_log = jnp.maximum(value, 0.0) + log_one
                square = factor * (prob * prob)
                loss = loss + (jnp.abs(square) * neg_log).reshape(step // 8, 8, TILE).sum(0)
                other_log = other * neg_log
                d_logit = square * (prob + (other_log + other_log))
                d_shift = d_shift + d_logit.reshape(step // 8, 8, TILE).sum(0)
                d_scale = d_scale + (d_logit * base).reshape(step // 8, 8, TILE).sum(0)
                grads[rows, cols] = (d_logit * scale).astype(BF16)
                return loss, d_shift, d_scale

            zero = jnp.zeros((8, TILE), F32)
            loss, d_shift, d_scale = lax.fori_loop(0, Q // step, block, (loss_sum, zero, zero))
            d_rows[0:1, cols] = jnp.sum(d_shift, axis=0, keepdims=True)
            d_rows[1:2, cols] = jnp.sum(d_scale, axis=0, keepdims=True) * jnp.where(
                pre > 0, 1.0, decay
            )
            return loss

        return lax.fori_loop(0, BLOCK // TILE, tile, loss_sum)

    focal_sum = lax.fori_loop(0, ROWS // BLOCK, focal, jnp.zeros((8, TILE), F32))

    def embedding_grad(i, carry):
        rows = rows_of(i, BLOCK)
        d_units = contract(grads[:, rows], unit_q[...], 0, 0)
        unit = exact[rows, :]
        along = jnp.sum(unit * d_units, axis=1, keepdims=True)
        d_emb[rows, :] = ((d_units - unit * along) * inv_norm[rows, :]).astype(BF16)
        return carry

    lax.fori_loop(0, ROWS // BLOCK, embedding_grad, 0)

    def pair_copy(k):
        return remote(g_both.at[1 - core, k], g_recv.at[k], gp_ssem.at[k], gp_rsem.at[k], pair)

    def y1_copy(k, d):
        return remote(s0.at[(y + d) % NY, k], r1y.at[d - 1, k], y1_ssem.at[d - 1, k], y1_rsem.at[d - 1, k], y_peer(d))

    def x1_copy(k, d):
        return remote(s1.at[(x + d) % NX, k], r1x.at[d - 1, k], x1_ssem.at[d - 1, k], x1_rsem.at[d - 1, k], x_peer(d))

    def z_copy(half, k, h):
        distance = (k + NX * h - z + NZ) % NZ
        slot = jnp.maximum(distance - 1, 0)
        source, target, ssem, rsem = ((t0, r2a, z0_ssem, z0_rsem), (t1, r2b, z1_ssem, z1_rsem))[half]
        return distance, remote(
            source.at[k, h], target.at[slot], ssem.at[k, h], rsem.at[slot], z_peer(distance)
        )

    def produce(k):
        left = jnp.concatenate(
            [feat[:, k * 128 : (k + 1) * 128], feat[:, (k + NX) * 128 : (k + NX + 1) * 128]], axis=1
        )
        part = contract(left, d_emb[...], 0, 0).astype(BF16).reshape(2, NY, NC, SHARE, D)
        for cc in range(NC):
            g_both[cc, k] = part[:, :, cc]
        pair_copy(k).start()

    def consume(k):
        pair_copy(k).wait_recv()
        for h in range(2):
            both = (g_both[core, k, h].astype(F32) + g_recv[k, h].astype(F32)).astype(BF16)
            for yy in range(NY):
                s0[yy, k, h] = both[yy, :, 0:HALF]
                s1[yy, k, h] = both[yy, :, HALF:D]
        for d in ys:
            y1_copy(k, d).start()
        for d in xs:
            x1_copy(k, d).start()

    def forward(k):
        for half in range(2):
            own, got, copy, mine = ((s0, r1y, y1_copy, y), (s1, r1x, x1_copy, x))[half]
            total = own[mine, k].astype(F32)
            for d in ys:
                copy(k, d).wait_recv()
                total = total + got[d - 1, k].astype(F32)
            (t0, t1)[half][k] = total.astype(BF16)
            for h in range(2):
                distance, move = z_copy(half, k, h)
                pl.when(distance != 0)(move.start)

    produce(0)
    produce(1)
    consume(0)
    produce(2)
    consume(1)
    produce(3)
    consume(2)

    for n in range(D // TILE):
        cols = slice(n * TILE, (n + 1) * TILE)
        part = contract(grads[...], units[:, cols], 1, 0).astype(BF16)
        for g in range(NX):
            q_send[g, :, cols] = part[g * QROWS : (g + 1) * QROWS, :]
    consume(3)
    qs_copies = [
        remote(q_send.at[(x + d) % NX], q_recv.at[d - 1], qs_ssem.at[d - 1], qs_rsem.at[d - 1], x_peer(d))
        for d in xs
    ]
    for copy in qs_copies:
        copy.start()

    small[4:6, :] = contract(d_rows[...].astype(BF16), feat[...], 1, 0)
    fold = lambda row: row[:, 0:512] + row[:, 512:1024] + row[:, 1024:1536]
    focal_row = jnp.sum(focal_sum, axis=0, keepdims=True)
    small[6:7, 0:512] = GIOU_WEIGHT * fold(terms)
    small[6:7, 0:TILE] += focal_row
    small[6:7, 512:1024] = fold(weight)
    small[7:8, :] = jnp.zeros((1, E), F32)
    small_pair = remote(small, small_p, sp_sem.at[0], sp_sem.at[1], pair)
    small_pair.start()

    forward(0)
    small_pair.wait()
    for k in range(NZ):
        lanes = slice(k * 128, (k + 1) * 128)
        small_two[k] = small[:, lanes] + small_p[:, lanes]
    sz_copies = [
        remote(small_two.at[(z + d) % NZ], small_z.at[d - 1], sz_ssem.at[d - 1], sz_rsem.at[d - 1], z_peer(d))
        for d in zs
    ]
    for copy in sz_copies:
        copy.start()
    for k in range(1, NX):
        forward(k)

    for copy in sz_copies:
        copy.wait_recv()
    small_v[...] = (
        ((small_two[z] + small_z[0]) + (small_z[1] + small_z[2]))
        + ((small_z[3] + small_z[4]) + (small_z[5] + small_z[6]))
    )
    sxy_copies = [
        remote(small_v, small_xy.at[dy, dx], sxy_ssem.at[dy, dx], sxy_rsem.at[dy, dx], xy_peer(dy, dx))
        for dy, dx in plane
    ]
    for copy in sxy_copies:
        copy.start()

    def over_z(total, got, half):
        for d in zs:
            remote(t0.at[0, 0], got.at[d - 1], z0_ssem.at[0, 0], (z0_rsem, z1_rsem)[half].at[d - 1], z_peer(d)).wait_recv()
            total = total + got[d - 1].astype(F32)
        return total.astype(BF16)

    u0[...] = over_z(t0[z % NX, z // NX].astype(F32), r2a, 0)
    f0_copies = [remote(u0, r3a.at[d - 1], f0_ssem.at[d - 1], f0_rsem.at[d - 1], x_peer(d)) for d in xs]
    for copy in f0_copies:
        copy.start()
    u1[...] = over_z(t1[z % NX, z // NX].astype(F32), r2b, 1)

    def f1_copy(target):
        return remote(u1, r3b.at[y], f1_ssem.at[target], f1_rsem.at[y], at(z, x, core, target))

    for target in range(NX):
        itself = jnp.logical_and(y == x, x == target)
        pl.when(jnp.logical_not(itself))(f1_copy(target).start)

    @pl.when(y == x)
    def _():
        r3b[y] = u1[...]

    for copy in sxy_copies:
        copy.wait_recv()
    small_xy[0, 0] = small_v[...]
    line = [
        (small_xy[dy, 0] + small_xy[dy, 2]) + (small_xy[dy, 1] + small_xy[dy, 3]) for dy in range(NY)
    ]
    small_sum[...] = (line[0] + line[2]) + (line[1] + line[3])
    small_all[z] = small_sum[...]
    sa_copies = [
        remote(small_sum, small_all.at[z], sa_ssem.at[d - 1], sa_rsem.at[d - 1], z_peer(d)) for d in zs
    ]
    for copy in sa_copies:
        copy.start()

    for copy in qs_copies:
        copy.wait_recv()
    sums = q_send[x].astype(F32)
    for d in xs:
        sums = sums + q_recv[d - 1].astype(F32)
    mine = own_q[...].astype(F32)
    inv = lax.rsqrt(jnp.sum(mine * mine, axis=1, keepdims=True) + EPSILON)
    mine = mine * inv
    along = jnp.sum(mine * sums, axis=1, keepdims=True)
    query_raw = (sums - mine * along) * inv

    for copy in sa_copies:
        copy.wait_recv()
    for k in range(NZ):
        small[:, k * 128 : (k + 1) * 128] = small_all[k]
    per = 1.0 / jnp.sum(small[6:7, 512:1024], axis=1, keepdims=True)
    box_out[...] = small[0:4, :] * per
    side_out[...] = small[4:6, :] * per
    loss_out[...] = jnp.sum(small[6:7, 0:512], axis=1, keepdims=True) * per
    query_out[...] = query_raw * per

    for copy in f0_copies:
        copy.wait_recv()
    total = (u0[...].astype(F32) + r3a[1].astype(F32)) + (r3a[0].astype(F32) + r3a[2].astype(F32))
    class_out[:, 0:HALF] = total * per
    for source in range(NY):
        itself = jnp.logical_and(y == x, y == source)
        arrived = remote(u1, r3b.at[source], f1_ssem.at[0], f1_rsem.at[source], at(z, source, core, y))
        pl.when(jnp.logical_not(itself))(arrived.wait_recv)
    total = r3b[0].astype(F32)
    for source in range(1, NY):
        total = total + r3b[source].astype(F32)
    class_out[:, HALF:D] = total * per

    for k in range(NX):
        pair_copy(k).wait_send()
        for d in ys:
            y1_copy(k, d).wait_send()
            x1_copy(k, d).wait_send()
        for half in range(2):
            for h in range(2):
                distance, move = z_copy(half, k, h)
                pl.when(distance != 0)(move.wait_send)
    for copy in qs_copies + sz_copies + sxy_copies + sa_copies + f0_copies:
        copy.wait_send()
    for target in range(NX):
        itself = jnp.logical_and(y == x, x == target)
        pl.when(jnp.logical_not(itself))(f1_copy(target).wait_send)


def finish(*refs):
    count = len(refs) // 2
    for i in range(count):
        refs[count + i][...] = refs[i][...]


def on_device(features, targets, matches, queries, class_weight, trunk_weight, head_rows):
    hbm = pl.BlockSpec(memory_space=pl.ANY)
    vmem = pl.BlockSpec(memory_space=pltpu.VMEM)
    dma = lambda *shape: pltpu.SemaphoreType.DMA(shape)
    buf = lambda kind, *shape: pltpu.VMEM(shape, kind)
    loss, query, classes, box, side = pl.pallas_call(
        kernel,
        out_shape=(
            jax.ShapeDtypeStruct((1, 1), F32),
            jax.ShapeDtypeStruct((QROWS, D), F32),
            jax.ShapeDtypeStruct((SHARE, D), F32),
            jax.ShapeDtypeStruct((4, E), F32),
            jax.ShapeDtypeStruct((2, E), F32),
        ),
        in_specs=[hbm] * 4 + [vmem] * 4,
        out_specs=[vmem] * 5,
        scratch_shapes=[
            buf(BF16, ROWS, E),
            buf(BF16, E, D),
            buf(BF16, E, E),
            buf(BF16, QROWS, D),
            buf(BF16, NX, QROWS, D),
            buf(BF16, Q, D),
            buf(F32, ROWS, D),
            buf(F32, ROWS, 1),
            buf(BF16, ROWS, D),
            buf(BF16, ROWS, E),
            buf(F32, 6, ROWS),
            buf(F32, 6, ROWS),
            buf(F32, Q, BLOCK),
            buf(BF16, Q, ROWS),
            buf(F32, 2, ROWS),
            buf(BF16, ROWS, D),
            buf(F32, 8, E),
            buf(F32, 8, E),
            buf(F32, NZ, 8, 128),
            buf(F32, NZ - 1, 8, 128),
            buf(F32, 8, 128),
            buf(F32, NY, NX, 8, 128),
            buf(F32, 8, 128),
            buf(F32, NZ, 8, 128),
            buf(BF16, NX, QROWS, D),
            buf(BF16, NX - 1, QROWS, D),
            buf(BF16, NC, NX, 2, NY, SHARE, D),
            buf(BF16, NX, 2, NY, SHARE, D),
            buf(BF16, NY, NX, 2, SHARE, HALF),
            buf(BF16, NY, NX, 2, SHARE, HALF),
            buf(BF16, NY - 1, NX, 2, SHARE, HALF),
            buf(BF16, NX - 1, NX, 2, SHARE, HALF),
            buf(BF16, NX, 2, SHARE, HALF),
            buf(BF16, NX, 2, SHARE, HALF),
            buf(BF16, NZ - 1, SHARE, HALF),
            buf(BF16, NZ - 1, SHARE, HALF),
            buf(BF16, SHARE, HALF),
            buf(BF16, SHARE, HALF),
            buf(BF16, NX - 1, SHARE, HALF),
            buf(BF16, NY, SHARE, HALF),
            dma(4), dma(NX - 1), dma(NX - 1), dma(2),
            dma(NZ - 1), dma(NZ - 1), dma(NY, NX), dma(NY, NX),
            dma(NZ - 1), dma(NZ - 1), dma(NX - 1), dma(NX - 1), dma(NX), dma(NX),
            dma(NY - 1, NX), dma(NY - 1, NX), dma(NX - 1, NX), dma(NX - 1, NX),
            dma(NX, 2), dma(NZ - 1), dma(NX, 2), dma(NZ - 1),
            dma(NX - 1), dma(NX - 1), dma(NX), dma(NY),
        ],
        compiler_params=pltpu.CompilerParams(
            collective_id=0, has_side_effects=True, vmem_limit_bytes=56 * 1024 * 1024
        ),
        cost_estimate=pl.CostEstimate(
            flops=11_000_000_000, bytes_accessed=8_000_000, transcendentals=4_000_000
        ),
    )(
        queries, features, class_weight, trunk_weight, targets, matches, head_rows,
        jnp.asarray(box_prior(ROWS)),
    )
    results = (loss, query, classes, box, side)
    loss, query, classes, box, side = pl.pallas_call(
        finish,
        out_shape=tuple(jax.ShapeDtypeStruct(r.shape, F32) for r in results),
        in_specs=[vmem] * 5,
        out_specs=[vmem] * 5,
    )(*results)
    return loss[0, 0], query, classes, box, side


def solution(mesh):
    in_specs = (
        P(("dp", "group"), None, None),
        P(("dp", "group"), None, None),
        P(("dp", "group"), None),
        P(("dp", "group"), None),
        P(),
        P(),
        P(),
    )
    out_specs = (P(), P(("dp", "group"), None), P("dp", None), P(), P())
    return jax.shard_map(
        on_device, mesh=mesh, in_specs=in_specs, out_specs=out_specs, check_vma=False
    )
```

```python
import functools

import jax
import jax.numpy as jnp
import numpy as np
from jax import lax
from jax.experimental import pallas as pl
from jax.experimental.pallas import tpu as pltpu
from jax.sharding import PartitionSpec as P

MESH = pl.DeviceIdType.MESH
F32 = jnp.float32
BF16 = jnp.bfloat16

GRID = 72
QUANT = 1024
ALPHA = 0.25
GIOU_WEIGHT = 2.0
LOGIT_BIAS = -4.0
EPSILON = 1e-06
LOG2E = 1.4426950408889634

NX, NY, NZ, NC = 4, 4, 8, 2
E, D, ROWS, Q = 1024, 768, 1536, 384
QROWS = Q // NX
SHARE = E // (NZ * NY * NC)
HALF = D // 2
BLOCK = 768
TILE = 256
CHUNKS = ((0, 256), (256, 512), (768, 768))
ORDER = (0, 1, 3, 2)
EARLY = 3
PEERS = 1 + (NX * NY - 1) + (NZ - 1)


def contract(left, right, left_dim, right_dim):
    return lax.dot_general(
        left, right, (((left_dim,), (right_dim,)), ((), ())), preferred_element_type=F32
    )


def box_prior(length):
    index = np.arange(length)

    def logit(value):
        return np.log(value) - np.log1p(-value)

    across = logit((index % GRID + 0.5) / GRID)
    down = logit((index // GRID + 0.5) / GRID)
    size = np.full((length,), logit(1.0 / GRID))
    return np.stack([across, down, size, size], 0).astype(np.float32)


def box_loss(box_raw, corners, weight):
    box = jax.nn.sigmoid(box_raw)
    cx, cy, bw, bh = (box[i : i + 1] for i in range(4))
    c0, c1, c2, c3 = (corners[i : i + 1] for i in range(4))
    left = cx - 0.5 * bw
    right = cx + 0.5 * bw
    top = cy - 0.5 * bh
    bottom = cy + 0.5 * bh
    inter_w = jnp.maximum(jnp.minimum(right, c2) - jnp.maximum(left, c0), 0.0)
    inter_h = jnp.maximum(jnp.minimum(bottom, c3) - jnp.maximum(top, c1), 0.0)
    inter = inter_w * inter_h
    union = bw * bh + (c2 - c0) * (c3 - c1) - inter
    outer_w = jnp.maximum(right, c2) - jnp.minimum(left, c0)
    outer_h = jnp.maximum(bottom, c3) - jnp.minimum(top, c1)
    enclose = outer_w * outer_h
    giou = inter / union - (enclose - union) / enclose
    return weight * (1.0 - giou)


def gelu(value):
    inner = value * (0.7978845608028654 + 0.035677408136300125 * (value * value))
    half = 0.5 * value
    return half + half * jnp.tanh(inner)


def rows_of(index, size):
    return pl.ds(pl.multiple_of(index * size, size), size)


def kernel(
    queries_hbm, features_hbm, cw_hbm, tw_hbm, targets_hbm, matches_hbm, heads_hbm, prior_hbm,
    loss_out, query_out, class_out, box_out, side_out,
    targets_ref, matches_ref, heads_ref, prior_ref, feat, cw, tw, own_q, all_q, unit_q, exact, inv_norm, units, hidden, raw, side,
    cosine, grads, sum_shift, sum_scale, d_rows, d_emb, small, small_p, small_two, small_z, small_v, small_xy, small_sum,
    small_all, q_send, q_recv, g_both, g_recv, s0, s1, r1y, r1x, t0, t1, r2a, r2b, u0, u1, r3a, r3b,
    load_sem, q_ssem, q_rsem, sp_sem, sz_ssem, sz_rsem, sxy_ssem, sxy_rsem,
    sa_ssem, sa_rsem, qs_ssem, qs_rsem, gp_ssem, gp_rsem, y1_ssem, y1_rsem, x1_ssem, x1_rsem,
    z0_ssem, z0_rsem, z1_ssem, z1_rsem, f0_ssem, f0_rsem, f1_ssem, f1_rsem,
):
    dp = lax.axis_index("dp")
    x = lax.axis_index("group")
    core = dp % NC
    y = (dp // NC) % NY
    z = dp // (NC * NY)

    def at(zz, yy, cc, xx):
        return ((zz * NY + yy) * NC + cc, xx)

    pair = at(z, y, 1 - core, x)
    x_peer = lambda d: at(z, y, core, (x + d) % NX)
    y_peer = lambda d: at(z, (y + d) % NY, core, x)
    xy_peer = lambda dy, dx: at(z, (y + dy) % NY, core, (x + dx) % NX)
    z_peer = lambda d: at((z + d) % NZ, y, core, x)
    xs, ys, zs = range(1, NX), range(1, NY), range(1, NZ)
    plane = [(dy, dx) for dy in range(NY) for dx in range(NX) if dy or dx]

    def remote(src, dst, ssem, rsem, device):
        return pltpu.make_async_remote_copy(
            src_ref=src, dst_ref=dst, send_sem=ssem, recv_sem=rsem,
            device_id=device, device_id_type=MESH,
        )

    loads = [
        pltpu.make_async_copy(source, target, load_sem.at[i])
        for i, (source, target) in enumerate(
            [(cw_hbm, cw)]
            + [
                (features_hbm.at[0, pl.ds(start, size)], feat.at[pl.ds(start, size)])
                for start, size in CHUNKS
            ]
            + [
                (queries_hbm, own_q),
                (heads_hbm, heads_ref),
                (tw_hbm, tw),
                (prior_hbm, prior_ref),
                (targets_hbm.at[0], targets_ref),
                (matches_hbm, matches_ref),
            ]
        )
    ]
    for load in loads[:4]:
        load.start()

    barrier = pltpu.get_barrier_semaphore()
    peers = [pair] + [xy_peer(dy, dx) for dy, dx in plane] + [z_peer(d) for d in zs]
    for peer in peers:
        pl.semaphore_signal(barrier, inc=1, device_id=peer, device_id_type=MESH)
    def embed(start, size):
        rows = pl.ds(start, size)
        emb = contract(feat[rows, :], cw[...], 1, 0)
        inv = lax.rsqrt(jnp.sum(emb * emb, axis=1, keepdims=True) + EPSILON)
        unit = emb * inv
        exact[rows, :] = unit
        units[rows, :] = unit.astype(BF16)
        inv_norm[rows, :] = inv

    loads[0].wait()
    loads[1].wait()
    for load in loads[4:]:
        load.start()
    embed(*CHUNKS[0])
    loads[2].wait()
    embed(*CHUNKS[1])

    loads[4].wait()
    all_q[0] = own_q[...]
    pl.semaphore_wait(barrier, PEERS)
    q_copies = {
        d: remote(own_q, all_q.at[ORDER.index(NX - d)], q_ssem.at[d - 1], q_rsem.at[d - 1], x_peer(d))
        for d in (1, 3, 2)
    }
    for copy in q_copies.values():
        copy.start()
    loads[3].wait()
    embed(*CHUNKS[2])
    for load in loads[5:]:
        load.wait()

    def box_hidden(i, carry):
        rows = rows_of(i, BLOCK)
        block = feat[rows, :]
        hid = gelu(contract(block, tw[...], 1, 0)).astype(BF16)
        hidden[rows, :] = hid
        raw[:, rows] = contract(hid, heads_ref[...], 1, 1).T
        side[:, rows] = contract(block, heads_ref[...], 1, 1).T
        return carry

    lax.fori_loop(0, ROWS // BLOCK, box_hidden, 0)

    matches = matches_ref[...]
    weight = (matches >= 0).astype(F32)
    corners = targets_ref[...].astype(F32) * (1.0 / QUANT)
    terms, pullback = jax.vjp(
        lambda value: box_loss(value, corners, weight), raw[0:4, :] + prior_ref[...]
    )
    d_raw = (GIOU_WEIGHT * pullback(jnp.ones_like(terms))[0]).astype(BF16)
    small[0:4, :] = contract(d_raw, hidden[...], 1, 0)

    def normalise(slot):
        rows = all_q[slot].astype(F32)
        inv = lax.rsqrt(jnp.sum(rows * rows, axis=1, keepdims=True) + EPSILON)
        unit_q[slot * QROWS : (slot + 1) * QROWS, :] = (rows * inv).astype(BF16)

    step = 32

    def focal(first, last, i, loss_sum):
        rows = slice(first * QROWS, last * QROWS)
        cosine[rows, :] = contract(unit_q[rows, :], units[rows_of(i, BLOCK), :], 1, 1)

        def tile(n, loss_sum):
            cols = rows_of(i * (BLOCK // TILE) + n, TILE)
            here = rows_of(n, TILE)
            shift = side[4:5, cols] + LOGIT_BIAS
            pre = side[5:6, cols]
            decay = jnp.exp(jnp.minimum(pre, 0.0))
            scale = jnp.where(pre > 0, pre + 1.0, decay)
            scale_two = scale * LOG2E
            match = matches_ref[:, cols]

            def block(j, target, carry):
                loss, d_shift, d_scale = carry
                rows = rows_of(j, step)
                base = cosine[rows, here] + shift
                hit = lax.broadcasted_iota(jnp.int32, (step, TILE), 0) == target
                logit = base * scale_two
                value = jnp.where(hit, -logit, logit)
                factor = jnp.where(hit, -ALPHA, 1.0 - ALPHA)
                power = jnp.exp2(jnp.minimum(value, 100.0))
                log_one = jnp.where(
                    power < 2.0**-8, power * (LOG2E - power * (LOG2E / 2 - power * (LOG2E / 3))), jnp.log2(1.0 + power)
                )
                neg_log = jnp.maximum(log_one, value)
                prob = jnp.exp2(value - neg_log)
                other = jnp.exp2(-neg_log)
                square = factor * (prob * prob)
                loss = loss + (jnp.abs(square) * neg_log).reshape(step // 8, 8, TILE).sum(0)
                d_logit = square * (prob + (2.0 / LOG2E) * (other * neg_log))
                d_shift = d_shift + d_logit.reshape(step // 8, 8, TILE).sum(0)
                d_scale = d_scale + (d_logit * base).reshape(step // 8, 8, TILE).sum(0)
                grads[rows, cols] = (d_logit * scale).astype(BF16)
                return loss, d_shift, d_scale

            def query_block(slot, carry):
                owner = (x + slot + slot // 2 - 2 * (slot // 3)) % NX
                target = match - owner * QROWS
                for part in range(QROWS // step):
                    carry = block(slot * (QROWS // step) + part, target - part * step, carry)
                return carry

            if first:
                d_shift, d_scale = sum_shift[:, cols], sum_scale[:, cols]
            else:
                d_shift = d_scale = jnp.zeros((8, TILE), F32)
            loss, d_shift, d_scale = lax.fori_loop(
                first, last, query_block, (loss_sum, d_shift, d_scale)
            )
            sum_shift[:, cols], sum_scale[:, cols] = d_shift, d_scale
            return loss

        return lax.fori_loop(0, BLOCK // TILE, tile, loss_sum)

    q_copies[1].wait_recv()
    q_copies[3].wait_recv()
    q_copies[2].wait_recv()
    for slot in range(4):
        normalise(slot)
    focal_sum = lax.fori_loop(
        0, ROWS // BLOCK, functools.partial(focal, 0, NX), jnp.zeros((8, TILE), F32)
    )

    def embedding_grad(i, carry):
        rows = rows_of(i, BLOCK)
        d_units = contract(grads[:, rows], unit_q[...], 0, 0)
        unit = exact[rows, :]
        along = jnp.sum(unit * d_units, axis=1, keepdims=True)
        d_emb[rows, :] = ((d_units - unit * along) * inv_norm[rows, :]).astype(BF16)
        return carry

    lax.fori_loop(0, ROWS // BLOCK, embedding_grad, 0)

    def pair_copy(k):
        return remote(g_both.at[1 - core, k], g_recv.at[k], gp_ssem.at[k], gp_rsem.at[k], pair)

    def y1_copy(k, d):
        return remote(s0.at[(y + d) % NY, k], r1y.at[d - 1, k], y1_ssem.at[d - 1, k], y1_rsem.at[d - 1, k], y_peer(d))

    def x1_copy(k, d):
        return remote(s1.at[(x + d) % NX, k], r1x.at[d - 1, k], x1_ssem.at[d - 1, k], x1_rsem.at[d - 1, k], x_peer(d))

    def z_copy(half, k, h):
        distance = (k + NX * h - z + NZ) % NZ
        slot = jnp.maximum(distance - 1, 0)
        source, target, ssem, rsem = ((t0, r2a, z0_ssem, z0_rsem), (t1, r2b, z1_ssem, z1_rsem))[half]
        return distance, remote(
            source.at[k, h], target.at[slot], ssem.at[k, h], rsem.at[slot], z_peer(distance)
        )

    def produce(k):
        left = jnp.concatenate(
            [feat[:, k * 128 : (k + 1) * 128], feat[:, (k + NX) * 128 : (k + NX + 1) * 128]], axis=1
        )
        part = contract(left, d_emb[...], 0, 0).astype(BF16).reshape(2, NY, NC, SHARE, D)
        for cc in range(NC):
            g_both[cc, k] = part[:, :, cc]
        pair_copy(k).start()

    def consume(k):
        pair_copy(k).wait_recv()
        for h in range(2):
            both = (g_both[core, k, h].astype(F32) + g_recv[k, h].astype(F32)).astype(BF16)
            for yy in range(NY):
                s0[yy, k, h] = both[yy, :, 0:HALF]
                s1[yy, k, h] = both[yy, :, HALF:D]
        for d in ys:
            y1_copy(k, d).start()
        for d in xs:
            x1_copy(k, d).start()

    def forward(k):
        for half in range(2):
            own, got, copy, mine = ((s0, r1y, y1_copy, y), (s1, r1x, x1_copy, x))[half]
            total = own[mine, k].astype(F32)
            for d in ys:
                copy(k, d).wait_recv()
                total = total + got[d - 1, k].astype(F32)
            (t0, t1)[half][k] = total.astype(BF16)
            for h in range(2):
                distance, move = z_copy(half, k, h)
                pl.when(distance != 0)(move.start)

    produce(0)
    produce(1)
    consume(0)
    produce(2)
    consume(1)
    produce(3)
    consume(2)

    for n in range(D // TILE):
        cols = slice(n * TILE, (n + 1) * TILE)
        part = contract(grads[...], units[:, cols], 1, 0).astype(BF16)
        for g in range(NX):
            q_send[g, :, cols] = part[g * QROWS : (g + 1) * QROWS, :]
    consume(3)
    qs_copies = [
        remote(q_send.at[ORDER.index(d)], q_recv.at[d - 1], qs_ssem.at[d - 1], qs_rsem.at[d - 1], x_peer(d))
        for d in xs
    ]
    for copy in qs_copies:
        copy.start()

    pre = side[5:6, :]
    d_rows[0:1, :] = jnp.sum(sum_shift[...], axis=0, keepdims=True)
    d_rows[1:2, :] = jnp.sum(sum_scale[...], axis=0, keepdims=True) * jnp.where(
        pre > 0, 1.0, jnp.exp(jnp.minimum(pre, 0.0))
    )
    small[4:6, :] = contract(d_rows[...].astype(BF16), feat[...], 1, 0)
    fold = lambda row: row[:, 0:512] + row[:, 512:1024] + row[:, 1024:1536]
    focal_row = jnp.sum(focal_sum, axis=0, keepdims=True) * (1.0 / LOG2E)
    small[6:7, 0:512] = GIOU_WEIGHT * fold(terms)
    small[6:7, 0:TILE] += focal_row
    small[6:7, 512:1024] = fold(weight)
    small[7:8, :] = jnp.zeros((1, E), F32)
    small_pair = remote(small, small_p, sp_sem.at[0], sp_sem.at[1], pair)
    small_pair.start()

    forward(0)
    small_pair.wait()
    for k in range(NZ):
        lanes = slice(k * 128, (k + 1) * 128)
        small_two[k] = small[:, lanes] + small_p[:, lanes]
    sz_copies = [
        remote(small_two.at[(z + d) % NZ], small_z.at[d - 1], sz_ssem.at[d - 1], sz_rsem.at[d - 1], z_peer(d))
        for d in zs
    ]
    for copy in sz_copies:
        copy.start()
    for k in range(1, NX):
        forward(k)

    for copy in sz_copies:
        copy.wait_recv()
    small_v[...] = (
        ((small_two[z] + small_z[0]) + (small_z[1] + small_z[2]))
        + ((small_z[3] + small_z[4]) + (small_z[5] + small_z[6]))
    )
    sxy_copies = [
        remote(small_v, small_xy.at[dy, dx], sxy_ssem.at[dy, dx], sxy_rsem.at[dy, dx], xy_peer(dy, dx))
        for dy, dx in plane
    ]
    for copy in sxy_copies:
        copy.start()

    def over_z(total, got, half):
        for d in zs:
            remote(t0.at[0, 0], got.at[d - 1], z0_ssem.at[0, 0], (z0_rsem, z1_rsem)[half].at[d - 1], z_peer(d)).wait_recv()
            total = total + got[d - 1].astype(F32)
        return total.astype(BF16)

    u0[...] = over_z(t0[z % NX, z // NX].astype(F32), r2a, 0)
    f0_copies = [remote(u0, r3a.at[d - 1], f0_ssem.at[d - 1], f0_rsem.at[d - 1], x_peer(d)) for d in xs]
    for copy in f0_copies:
        copy.start()
    u1[...] = over_z(t1[z % NX, z // NX].astype(F32), r2b, 1)

    def f1_copy(target):
        return remote(u1, r3b.at[y], f1_ssem.at[target], f1_rsem.at[y], at(z, x, core, target))

    for target in range(NX):
        itself = jnp.logical_and(y == x, x == target)
        pl.when(jnp.logical_not(itself))(f1_copy(target).start)

    @pl.when(y == x)
    def _():
        r3b[y] = u1[...]

    for copy in sxy_copies:
        copy.wait_recv()
    small_xy[0, 0] = small_v[...]
    line = [
        (small_xy[dy, 0] + small_xy[dy, 2]) + (small_xy[dy, 1] + small_xy[dy, 3]) for dy in range(NY)
    ]
    small_sum[...] = (line[0] + line[2]) + (line[1] + line[3])
    small_all[z] = small_sum[...]
    sa_copies = [
        remote(small_sum, small_all.at[z], sa_ssem.at[d - 1], sa_rsem.at[d - 1], z_peer(d)) for d in zs
    ]
    for copy in sa_copies:
        copy.start()

    for copy in qs_copies:
        copy.wait_recv()
    sums = q_send[0].astype(F32)
    for d in xs:
        sums = sums + q_recv[d - 1].astype(F32)
    mine = own_q[...].astype(F32)
    inv = lax.rsqrt(jnp.sum(mine * mine, axis=1, keepdims=True) + EPSILON)
    mine = mine * inv
    along = jnp.sum(mine * sums, axis=1, keepdims=True)
    query_raw = (sums - mine * along) * inv

    for copy in sa_copies:
        copy.wait_recv()
    for k in range(NZ):
        small[:, k * 128 : (k + 1) * 128] = small_all[k]
    per = 1.0 / jnp.sum(small[6:7, 512:1024], axis=1, keepdims=True)
    box_out[...] = small[0:4, :] * per
    side_out[...] = small[4:6, :] * per
    loss_out[...] = jnp.sum(small[6:7, 0:512], axis=1, keepdims=True) * per
    query_out[...] = query_raw * per

    for copy in f0_copies:
        copy.wait_recv()
    total = (u0[...].astype(F32) + r3a[1].astype(F32)) + (r3a[0].astype(F32) + r3a[2].astype(F32))
    class_out[:, 0:HALF] = total * per
    for source in range(NY):
        itself = jnp.logical_and(y == x, y == source)
        arrived = remote(u1, r3b.at[source], f1_ssem.at[0], f1_rsem.at[source], at(z, source, core, y))
        pl.when(jnp.logical_not(itself))(arrived.wait_recv)
    total = r3b[0].astype(F32)
    for source in range(1, NY):
        total = total + r3b[source].astype(F32)
    class_out[:, HALF:D] = total * per

    for k in range(NX):
        pair_copy(k).wait_send()
        for d in ys:
            y1_copy(k, d).wait_send()
            x1_copy(k, d).wait_send()
        for half in range(2):
            for h in range(2):
                distance, move = z_copy(half, k, h)
                pl.when(distance != 0)(move.wait_send)
    for copy in list(q_copies.values()) + qs_copies + sz_copies + sxy_copies + sa_copies + f0_copies:
        copy.wait_send()
    for target in range(NX):
        itself = jnp.logical_and(y == x, x == target)
        pl.when(jnp.logical_not(itself))(f1_copy(target).wait_send)


def finish(*refs):
    count = len(refs) // 2
    for i in range(count):
        refs[count + i][...] = refs[i][...]


def on_device(features, targets, matches, queries, class_weight, trunk_weight, head_rows):
    hbm = pl.BlockSpec(memory_space=pl.ANY)
    vmem = pl.BlockSpec(memory_space=pltpu.VMEM)
    dma = lambda *shape: pltpu.SemaphoreType.DMA(shape)
    buf = lambda kind, *shape: pltpu.VMEM(shape, kind)
    loss, query, classes, box, side = pl.pallas_call(
        kernel,
        out_shape=(
            jax.ShapeDtypeStruct((1, 1), F32),
            jax.ShapeDtypeStruct((QROWS, D), F32),
            jax.ShapeDtypeStruct((SHARE, D), F32),
            jax.ShapeDtypeStruct((4, E), F32),
            jax.ShapeDtypeStruct((2, E), F32),
        ),
        in_specs=[hbm] * 8,
        out_specs=[vmem] * 5,
        scratch_shapes=[
            buf(jnp.int32, 4, ROWS),
            buf(jnp.int32, 1, ROWS),
            buf(BF16, 6, E),
            buf(F32, 4, ROWS),
            buf(BF16, ROWS, E),
            buf(BF16, E, D),
            buf(BF16, E, E),
            buf(BF16, QROWS, D),
            buf(BF16, NX, QROWS, D),
            buf(BF16, Q, D),
            buf(F32, ROWS, D),
            buf(F32, ROWS, 1),
            buf(BF16, ROWS, D),
            buf(BF16, ROWS, E),
            buf(F32, 6, ROWS),
            buf(F32, 6, ROWS),
            buf(F32, Q, BLOCK),
            buf(BF16, Q, ROWS),
            buf(F32, 8, ROWS),
            buf(F32, 8, ROWS),
            buf(F32, 2, ROWS),
            buf(BF16, ROWS, D),
            buf(F32, 8, E),
            buf(F32, 8, E),
            buf(F32, NZ, 8, 128),
            buf(F32, NZ - 1, 8, 128),
            buf(F32, 8, 128),
            buf(F32, NY, NX, 8, 128),
            buf(F32, 8, 128),
            buf(F32, NZ, 8, 128),
            buf(BF16, NX, QROWS, D),
            buf(BF16, NX - 1, QROWS, D),
            buf(BF16, NC, NX, 2, NY, SHARE, D),
            buf(BF16, NX, 2, NY, SHARE, D),
            buf(BF16, NY, NX, 2, SHARE, HALF),
            buf(BF16, NY, NX, 2, SHARE, HALF),
            buf(BF16, NY - 1, NX, 2, SHARE, HALF),
            buf(BF16, NX - 1, NX, 2, SHARE, HALF),
            buf(BF16, NX, 2, SHARE, HALF),
            buf(BF16, NX, 2, SHARE, HALF),
            buf(BF16, NZ - 1, SHARE, HALF),
            buf(BF16, NZ - 1, SHARE, HALF),
            buf(BF16, SHARE, HALF),
            buf(BF16, SHARE, HALF),
            buf(BF16, NX - 1, SHARE, HALF),
            buf(BF16, NY, SHARE, HALF),
            dma(10), dma(NX - 1), dma(NX - 1), dma(2),
            dma(NZ - 1), dma(NZ - 1), dma(NY, NX), dma(NY, NX),
            dma(NZ - 1), dma(NZ - 1), dma(NX - 1), dma(NX - 1), dma(NX), dma(NX),
            dma(NY - 1, NX), dma(NY - 1, NX), dma(NX - 1, NX), dma(NX - 1, NX),
            dma(NX, 2), dma(NZ - 1), dma(NX, 2), dma(NZ - 1),
            dma(NX - 1), dma(NX - 1), dma(NX), dma(NY),
        ],
        compiler_params=pltpu.CompilerParams(
            collective_id=0, has_side_effects=True, vmem_limit_bytes=56 * 1024 * 1024
        ),
        cost_estimate=pl.CostEstimate(
            flops=11_000_000_000, bytes_accessed=8_000_000, transcendentals=4_000_000
        ),
    )(
        queries, features, class_weight, trunk_weight, targets, matches, head_rows,
        jnp.asarray(box_prior(ROWS)),
    )
    results = (loss, query, classes, box, side)
    loss, query, classes, box, side = pl.pallas_call(
        finish,
        out_shape=tuple(jax.ShapeDtypeStruct(r.shape, F32) for r in results),
        in_specs=[vmem] * 5,
        out_specs=[vmem] * 5,
    )(*results)
    return loss[0, 0], query, classes, box, side


def solution(mesh):
    in_specs = (
        P(("dp", "group"), None, None),
        P(("dp", "group"), None, None),
        P(("dp", "group"), None),
        P(("dp", "group"), None),
        P(),
        P(),
        P(),
    )
    out_specs = (P(), P(("dp", "group"), None), P("dp", None), P(), P())
    return jax.shard_map(
        on_device, mesh=mesh, in_specs=in_specs, out_specs=out_specs, check_vma=False
    )
```

```python
import functools

import jax
import jax.numpy as jnp
import numpy as np
from jax import lax
from jax.experimental import pallas as pl
from jax.experimental.pallas import tpu as pltpu
from jax.sharding import PartitionSpec as P

MESH = pl.DeviceIdType.MESH
F32 = jnp.float32
BF16 = jnp.bfloat16

GRID = 72
QUANT = 1024
ALPHA = 0.25
GIOU_WEIGHT = 2.0
LOGIT_BIAS = -4.0
EPSILON = 1e-06
LOG2E = 1.4426950408889634

NX, NY, NZ, NC = 4, 4, 8, 2
E, D, ROWS, Q = 1024, 768, 1536, 384
QROWS = Q // NX
SHARE = E // (NZ * NY * NC)
HALF = D // 2
BLOCK = 768
TILE = 256
CHUNKS = ((0, 256), (256, 512), (768, 768))
ORDER = (0, 1, 3, 2)
EARLY = 3
PEERS = 1 + (NX * NY - 1) + (NZ - 1)


def contract(left, right, left_dim, right_dim):
    return lax.dot_general(
        left, right, (((left_dim,), (right_dim,)), ((), ())), preferred_element_type=F32
    )


def box_prior(length):
    index = np.arange(length)

    def logit(value):
        return np.log(value) - np.log1p(-value)

    across = logit((index % GRID + 0.5) / GRID)
    down = logit((index // GRID + 0.5) / GRID)
    size = np.full((length,), logit(1.0 / GRID))
    return np.stack([across, down, size, size], 0).astype(np.float32)


def box_loss(box_raw, corners, weight):
    box = jax.nn.sigmoid(box_raw)
    cx, cy, bw, bh = (box[i : i + 1] for i in range(4))
    c0, c1, c2, c3 = (corners[i : i + 1] for i in range(4))
    left = cx - 0.5 * bw
    right = cx + 0.5 * bw
    top = cy - 0.5 * bh
    bottom = cy + 0.5 * bh
    inter_w = jnp.maximum(jnp.minimum(right, c2) - jnp.maximum(left, c0), 0.0)
    inter_h = jnp.maximum(jnp.minimum(bottom, c3) - jnp.maximum(top, c1), 0.0)
    inter = inter_w * inter_h
    union = bw * bh + (c2 - c0) * (c3 - c1) - inter
    outer_w = jnp.maximum(right, c2) - jnp.minimum(left, c0)
    outer_h = jnp.maximum(bottom, c3) - jnp.minimum(top, c1)
    enclose = outer_w * outer_h
    giou = inter / union - (enclose - union) / enclose
    return weight * (1.0 - giou)


def gelu(value):
    inner = value * (0.7978845608028654 + 0.035677408136300125 * (value * value))
    half = 0.5 * value
    return half + half * jnp.tanh(inner)


def rows_of(index, size):
    return pl.ds(pl.multiple_of(index * size, size), size)


def kernel(
    queries_hbm, features_hbm, cw_hbm, tw_hbm, targets_hbm, matches_hbm, heads_hbm, prior_hbm,
    loss_out, query_out, class_out, box_out, side_out,
    targets_ref, matches_ref, heads_ref, prior_ref, feat, cw, tw, own_q, all_q, unit_q, exact, inv_norm, units, hidden, raw, side,
    cosine, grads, sum_shift, sum_scale, d_rows, d_emb, small, small_p, small_two, small_z, small_v, small_xy, small_sum,
    small_all, q_send, q_recv, g_both, g_recv, s0, s1, r1y, r1x, t0, t1, r2a, r2b, u0, u1, r3a, r3b,
    load_sem, q_ssem, q_rsem, sp_sem, sz_ssem, sz_rsem, sxy_ssem, sxy_rsem,
    sa_ssem, sa_rsem, qs_ssem, qs_rsem, gp_ssem, gp_rsem, y1_ssem, y1_rsem, x1_ssem, x1_rsem,
    z0_ssem, z0_rsem, z1_ssem, z1_rsem, f0_ssem, f0_rsem, f1_ssem, f1_rsem,
):
    dp = lax.axis_index("dp")
    x = lax.axis_index("group")
    core = dp % NC
    y = (dp // NC) % NY
    z = dp // (NC * NY)

    def at(zz, yy, cc, xx):
        return ((zz * NY + yy) * NC + cc, xx)

    pair = at(z, y, 1 - core, x)
    x_peer = lambda d: at(z, y, core, (x + d) % NX)
    y_peer = lambda d: at(z, (y + d) % NY, core, x)
    xy_peer = lambda dy, dx: at(z, (y + dy) % NY, core, (x + dx) % NX)
    z_peer = lambda d: at((z + d) % NZ, y, core, x)
    xs, ys, zs = range(1, NX), range(1, NY), range(1, NZ)
    plane = [(dy, dx) for dy in range(NY) for dx in range(NX) if dy or dx]

    def remote(src, dst, ssem, rsem, device):
        return pltpu.make_async_remote_copy(
            src_ref=src, dst_ref=dst, send_sem=ssem, recv_sem=rsem,
            device_id=device, device_id_type=MESH,
        )

    loads = [
        pltpu.make_async_copy(source, target, load_sem.at[i])
        for i, (source, target) in enumerate(
            [(cw_hbm, cw)]
            + [
                (features_hbm.at[0, pl.ds(start, size)], feat.at[pl.ds(start, size)])
                for start, size in CHUNKS
            ]
            + [
                (queries_hbm, own_q),
                (heads_hbm, heads_ref),
                (tw_hbm, tw),
                (prior_hbm, prior_ref),
                (targets_hbm.at[0], targets_ref),
                (matches_hbm, matches_ref),
            ]
        )
    ]
    for load in loads[:4]:
        load.start()

    barrier = pltpu.get_barrier_semaphore()
    peers = [pair] + [xy_peer(dy, dx) for dy, dx in plane] + [z_peer(d) for d in zs]
    for peer in peers:
        pl.semaphore_signal(barrier, inc=1, device_id=peer, device_id_type=MESH)
    def embed(start, size):
        rows = pl.ds(start, size)
        emb = contract(feat[rows, :], cw[...], 1, 0)
        inv = lax.rsqrt(jnp.sum(emb * emb, axis=1, keepdims=True) + EPSILON)
        unit = emb * inv
        exact[rows, :] = unit
        units[rows, :] = unit.astype(BF16)
        inv_norm[rows, :] = inv

    loads[0].wait()
    loads[1].wait()
    for load in loads[4:]:
        load.start()
    embed(*CHUNKS[0])
    loads[2].wait()
    embed(*CHUNKS[1])

    loads[4].wait()
    all_q[0] = own_q[...]
    pl.semaphore_wait(barrier, PEERS)
    q_copies = {
        d: remote(own_q, all_q.at[ORDER.index(NX - d)], q_ssem.at[d - 1], q_rsem.at[d - 1], x_peer(d))
        for d in (1, 3, 2)
    }
    for copy in q_copies.values():
        copy.start()
    loads[3].wait()
    embed(*CHUNKS[2])
    for load in loads[5:]:
        load.wait()

    def box_hidden(i, carry):
        rows = rows_of(i, BLOCK)
        block = feat[rows, :]
        hid = gelu(contract(block, tw[...], 1, 0)).astype(BF16)
        hidden[rows, :] = hid
        raw[:, rows] = contract(hid, heads_ref[...], 1, 1).T
        side[:, rows] = contract(block, heads_ref[...], 1, 1).T
        return carry

    lax.fori_loop(0, ROWS // BLOCK, box_hidden, 0)

    matches = matches_ref[...]
    weight = (matches >= 0).astype(F32)
    corners = targets_ref[...].astype(F32) * (1.0 / QUANT)
    terms, pullback = jax.vjp(
        lambda value: box_loss(value, corners, weight), raw[0:4, :] + prior_ref[...]
    )
    d_raw = (GIOU_WEIGHT * pullback(jnp.ones_like(terms))[0]).astype(BF16)
    small[0:4, :] = contract(d_raw, hidden[...], 1, 0)

    def normalise(slot):
        rows = all_q[slot].astype(F32)
        inv = lax.rsqrt(jnp.sum(rows * rows, axis=1, keepdims=True) + EPSILON)
        unit_q[slot * QROWS : (slot + 1) * QROWS, :] = (rows * inv).astype(BF16)

    step = 32

    def focal(first, last, i, loss_sum):
        rows = slice(first * QROWS, last * QROWS)
        cosine[rows, :] = contract(unit_q[rows, :], units[rows_of(i, BLOCK), :], 1, 1)

        def tile(n, loss_sum):
            cols = rows_of(i * (BLOCK // TILE) + n, TILE)
            here = rows_of(n, TILE)
            shift = side[4:5, cols] + LOGIT_BIAS
            pre = side[5:6, cols]
            decay = jnp.exp(jnp.minimum(pre, 0.0))
            scale = jnp.where(pre > 0, pre + 1.0, decay)
            scale_two = scale * LOG2E
            match = matches_ref[:, cols]

            def block(j, target, carry):
                loss, d_shift, d_scale = carry
                rows = rows_of(j, step)
                base = cosine[rows, here] + shift
                hit = lax.broadcasted_iota(jnp.int32, (step, TILE), 0) == target
                logit = base * scale_two
                value = jnp.where(hit, -logit, logit)
                factor = jnp.where(hit, -ALPHA, 1.0 - ALPHA)
                power = jnp.exp2(jnp.minimum(value, 100.0))
                log_one = jnp.where(
                    power < 2.0**-8, power * (LOG2E - power * (LOG2E / 2 - power * (LOG2E / 3))), jnp.log2(1.0 + power)
                )
                neg_log = jnp.maximum(log_one, value)
                prob = jnp.exp2(value - neg_log)
                other = jnp.exp2(-neg_log)
                square = factor * (prob * prob)
                loss = loss + (jnp.abs(square) * neg_log).reshape(step // 8, 8, TILE).sum(0)
                d_logit = square * (prob + (2.0 / LOG2E) * (other * neg_log))
                d_shift = d_shift + d_logit.reshape(step // 8, 8, TILE).sum(0)
                d_scale = d_scale + (d_logit * base).reshape(step // 8, 8, TILE).sum(0)
                grads[rows, cols] = (d_logit * scale).astype(BF16)
                return loss, d_shift, d_scale

            def query_block(slot, carry):
                owner = (x + slot + slot // 2 - 2 * (slot // 3)) % NX
                target = match - owner * QROWS
                for part in range(QROWS // step):
                    carry = block(slot * (QROWS // step) + part, target - part * step, carry)
                return carry

            if first:
                d_shift, d_scale = sum_shift[:, cols], sum_scale[:, cols]
            else:
                d_shift = d_scale = jnp.zeros((8, TILE), F32)
            loss, d_shift, d_scale = lax.fori_loop(
                first, last, query_block, (loss_sum, d_shift, d_scale)
            )
            sum_shift[:, cols], sum_scale[:, cols] = d_shift, d_scale
            return loss

        return lax.fori_loop(0, BLOCK // TILE, tile, loss_sum)

    q_copies[1].wait_recv()
    q_copies[3].wait_recv()
    q_copies[2].wait_recv()
    for slot in range(4):
        normalise(slot)
    focal_sum = lax.fori_loop(
        0, ROWS // BLOCK, functools.partial(focal, 0, NX), jnp.zeros((8, TILE), F32)
    )

    def embedding_grad(i, carry):
        rows = rows_of(i, BLOCK)
        d_units = contract(grads[:, rows], unit_q[...], 0, 0)
        unit = exact[rows, :]
        along = jnp.sum(unit * d_units, axis=1, keepdims=True)
        d_emb[rows, :] = ((d_units - unit * along) * inv_norm[rows, :]).astype(BF16)
        return carry

    lax.fori_loop(0, ROWS // BLOCK, embedding_grad, 0)

    def pair_copy(k):
        return remote(g_both.at[1 - core, k], g_recv.at[k], gp_ssem.at[k], gp_rsem.at[k], pair)

    def y1_copy(k, d):
        return remote(s0.at[(y + d) % NY, k], r1y.at[d - 1, k], y1_ssem.at[d - 1, k], y1_rsem.at[d - 1, k], y_peer(d))

    def x1_copy(k, d):
        return remote(s1.at[(x + d) % NX, k], r1x.at[d - 1, k], x1_ssem.at[d - 1, k], x1_rsem.at[d - 1, k], x_peer(d))

    def z_copy(half, k, h):
        distance = (k + NX * h - z + NZ) % NZ
        slot = jnp.maximum(distance - 1, 0)
        source, target, ssem, rsem = ((t0, r2a, z0_ssem, z0_rsem), (t1, r2b, z1_ssem, z1_rsem))[half]
        return distance, remote(
            source.at[k, h], target.at[slot], ssem.at[k, h], rsem.at[slot], z_peer(distance)
        )

    def produce(k):
        left = jnp.concatenate(
            [feat[:, k * 128 : (k + 1) * 128], feat[:, (k + NX) * 128 : (k + NX + 1) * 128]], axis=1
        )
        part = contract(left, d_emb[...], 0, 0).astype(BF16).reshape(2, NY, NC, SHARE, D)
        for cc in range(NC):
            g_both[cc, k] = part[:, :, cc]
        pair_copy(k).start()

    def consume(k):
        pair_copy(k).wait_recv()
        for h in range(2):
            both = (g_both[core, k, h].astype(F32) + g_recv[k, h].astype(F32)).astype(BF16)
            for yy in range(NY):
                s0[yy, k, h] = both[yy, :, 0:HALF]
                s1[yy, k, h] = both[yy, :, HALF:D]
        for d in ys:
            y1_copy(k, d).start()
        for d in xs:
            x1_copy(k, d).start()

    def forward(k):
        for half in range(2):
            own, got, copy, mine = ((s0, r1y, y1_copy, y), (s1, r1x, x1_copy, x))[half]
            total = own[mine, k].astype(F32)
            for d in ys:
                copy(k, d).wait_recv()
                total = total + got[d - 1, k].astype(F32)
            (t0, t1)[half][k] = total.astype(BF16)
            for h in range(2):
                distance, move = z_copy(half, k, h)
                pl.when(distance != 0)(move.start)

    produce(0)
    produce(1)
    consume(0)
    produce(2)
    consume(1)
    produce(3)
    consume(2)

    pre = side[5:6, :]
    d_rows[0:1, :] = jnp.sum(sum_shift[...], axis=0, keepdims=True)
    d_rows[1:2, :] = jnp.sum(sum_scale[...], axis=0, keepdims=True) * jnp.where(
        pre > 0, 1.0, jnp.exp(jnp.minimum(pre, 0.0))
    )
    small[4:6, :] = contract(d_rows[...].astype(BF16), feat[...], 1, 0)
    fold = lambda row: row[:, 0:512] + row[:, 512:1024] + row[:, 1024:1536]
    focal_row = jnp.sum(focal_sum, axis=0, keepdims=True) * (1.0 / LOG2E)
    small[6:7, 0:512] = GIOU_WEIGHT * fold(terms)
    small[6:7, 0:TILE] += focal_row
    small[6:7, 512:1024] = fold(weight)
    small[7:8, :] = jnp.zeros((1, E), F32)
    small_pair = remote(small, small_p, sp_sem.at[0], sp_sem.at[1], pair)
    small_pair.start()

    consume(3)
    small_pair.wait()
    for k in range(NZ):
        lanes = slice(k * 128, (k + 1) * 128)
        small_two[k] = small[:, lanes] + small_p[:, lanes]
    sz_copies = [
        remote(small_two.at[(z + d) % NZ], small_z.at[d - 1], sz_ssem.at[d - 1], sz_rsem.at[d - 1], z_peer(d))
        for d in zs
    ]
    for copy in sz_copies:
        copy.start()
    for n in range(D // TILE):
        cols = slice(n * TILE, (n + 1) * TILE)
        part = contract(grads[...], units[:, cols], 1, 0).astype(BF16)
        for g in range(NX):
            q_send[g, :, cols] = part[g * QROWS : (g + 1) * QROWS, :]
    qs_copies = [
        remote(q_send.at[ORDER.index(d)], q_recv.at[d - 1], qs_ssem.at[d - 1], qs_rsem.at[d - 1], x_peer(d))
        for d in xs
    ]
    for copy in qs_copies:
        copy.start()

    for k in range(NX):
        forward(k)
    for copy in sz_copies:
        copy.wait_recv()
    small_v[...] = (
        ((small_two[z] + small_z[0]) + (small_z[1] + small_z[2]))
        + ((small_z[3] + small_z[4]) + (small_z[5] + small_z[6]))
    )
    sxy_copies = [
        remote(small_v, small_xy.at[dy, dx], sxy_ssem.at[dy, dx], sxy_rsem.at[dy, dx], xy_peer(dy, dx))
        for dy, dx in plane
    ]
    for copy in sxy_copies:
        copy.start()

    def over_z(total, got, half):
        for d in zs:
            remote(t0.at[0, 0], got.at[d - 1], z0_ssem.at[0, 0], (z0_rsem, z1_rsem)[half].at[d - 1], z_peer(d)).wait_recv()
            total = total + got[d - 1].astype(F32)
        return total.astype(BF16)

    u0[...] = over_z(t0[z % NX, z // NX].astype(F32), r2a, 0)
    f0_copies = [remote(u0, r3a.at[d - 1], f0_ssem.at[d - 1], f0_rsem.at[d - 1], x_peer(d)) for d in xs]
    for copy in f0_copies:
        copy.start()
    u1[...] = over_z(t1[z % NX, z // NX].astype(F32), r2b, 1)

    def f1_copy(target):
        return remote(u1, r3b.at[y], f1_ssem.at[target], f1_rsem.at[y], at(z, x, core, target))

    for target in range(NX):
        itself = jnp.logical_and(y == x, x == target)
        pl.when(jnp.logical_not(itself))(f1_copy(target).start)

    @pl.when(y == x)
    def _():
        r3b[y] = u1[...]

    for copy in sxy_copies:
        copy.wait_recv()
    small_xy[0, 0] = small_v[...]
    line = [
        (small_xy[dy, 0] + small_xy[dy, 2]) + (small_xy[dy, 1] + small_xy[dy, 3]) for dy in range(NY)
    ]
    small_sum[...] = (line[0] + line[2]) + (line[1] + line[3])
    small_all[z] = small_sum[...]
    sa_copies = [
        remote(small_sum, small_all.at[z], sa_ssem.at[d - 1], sa_rsem.at[d - 1], z_peer(d)) for d in zs
    ]
    for copy in sa_copies:
        copy.start()

    for copy in qs_copies:
        copy.wait_recv()
    sums = q_send[0].astype(F32)
    for d in xs:
        sums = sums + q_recv[d - 1].astype(F32)
    mine = own_q[...].astype(F32)
    inv = lax.rsqrt(jnp.sum(mine * mine, axis=1, keepdims=True) + EPSILON)
    mine = mine * inv
    along = jnp.sum(mine * sums, axis=1, keepdims=True)
    query_raw = (sums - mine * along) * inv

    for copy in sa_copies:
        copy.wait_recv()
    for k in range(NZ):
        small[:, k * 128 : (k + 1) * 128] = small_all[k]
    per = 1.0 / jnp.sum(small[6:7, 512:1024], axis=1, keepdims=True)
    box_out[...] = small[0:4, :] * per
    side_out[...] = small[4:6, :] * per
    loss_out[...] = jnp.sum(small[6:7, 0:512], axis=1, keepdims=True) * per
    query_out[...] = query_raw * per

    for copy in f0_copies:
        copy.wait_recv()
    total = (u0[...].astype(F32) + r3a[1].astype(F32)) + (r3a[0].astype(F32) + r3a[2].astype(F32))
    class_out[:, 0:HALF] = total * per
    for source in range(NY):
        itself = jnp.logical_and(y == x, y == source)
        arrived = remote(u1, r3b.at[source], f1_ssem.at[0], f1_rsem.at[source], at(z, source, core, y))
        pl.when(jnp.logical_not(itself))(arrived.wait_recv)
    total = r3b[0].astype(F32)
    for source in range(1, NY):
        total = total + r3b[source].astype(F32)
    class_out[:, HALF:D] = total * per

    for k in range(NX):
        pair_copy(k).wait_send()
        for d in ys:
            y1_copy(k, d).wait_send()
            x1_copy(k, d).wait_send()
        for half in range(2):
            for h in range(2):
                distance, move = z_copy(half, k, h)
                pl.when(distance != 0)(move.wait_send)
    for copy in list(q_copies.values()) + qs_copies + sz_copies + sxy_copies + sa_copies + f0_copies:
        copy.wait_send()
    for target in range(NX):
        itself = jnp.logical_and(y == x, x == target)
        pl.when(jnp.logical_not(itself))(f1_copy(target).wait_send)


def finish(*refs):
    count = len(refs) // 2
    for i in range(count):
        refs[count + i][...] = refs[i][...]


def on_device(features, targets, matches, queries, class_weight, trunk_weight, head_rows):
    hbm = pl.BlockSpec(memory_space=pl.ANY)
    vmem = pl.BlockSpec(memory_space=pltpu.VMEM)
    dma = lambda *shape: pltpu.SemaphoreType.DMA(shape)
    buf = lambda kind, *shape: pltpu.VMEM(shape, kind)
    loss, query, classes, box, side = pl.pallas_call(
        kernel,
        out_shape=(
            pltpu.VMEM((1, 1), F32),
            pltpu.VMEM((QROWS, D), F32),
            pltpu.VMEM((SHARE, D), F32),
            pltpu.VMEM((4, E), F32),
            pltpu.VMEM((2, E), F32),
        ),
        in_specs=[hbm] * 8,
        out_specs=[vmem] * 5,
        scratch_shapes=[
            buf(jnp.int32, 4, ROWS),
            buf(jnp.int32, 1, ROWS),
            buf(BF16, 6, E),
            buf(F32, 4, ROWS),
            buf(BF16, ROWS, E),
            buf(BF16, E, D),
            buf(BF16, E, E),
            buf(BF16, QROWS, D),
            buf(BF16, NX, QROWS, D),
            buf(BF16, Q, D),
            buf(F32, ROWS, D),
            buf(F32, ROWS, 1),
            buf(BF16, ROWS, D),
            buf(BF16, ROWS, E),
            buf(F32, 6, ROWS),
            buf(F32, 6, ROWS),
            buf(F32, Q, BLOCK),
            buf(BF16, Q, ROWS),
            buf(F32, 8, ROWS),
            buf(F32, 8, ROWS),
            buf(F32, 2, ROWS),
            buf(BF16, ROWS, D),
            buf(F32, 8, E),
            buf(F32, 8, E),
            buf(F32, NZ, 8, 128),
            buf(F32, NZ - 1, 8, 128),
            buf(F32, 8, 128),
            buf(F32, NY, NX, 8, 128),
            buf(F32, 8, 128),
            buf(F32, NZ, 8, 128),
            buf(BF16, NX, QROWS, D),
            buf(BF16, NX - 1, QROWS, D),
            buf(BF16, NC, NX, 2, NY, SHARE, D),
            buf(BF16, NX, 2, NY, SHARE, D),
            buf(BF16, NY, NX, 2, SHARE, HALF),
            buf(BF16, NY, NX, 2, SHARE, HALF),
            buf(BF16, NY - 1, NX, 2, SHARE, HALF),
            buf(BF16, NX - 1, NX, 2, SHARE, HALF),
            buf(BF16, NX, 2, SHARE, HALF),
            buf(BF16, NX, 2, SHARE, HALF),
            buf(BF16, NZ - 1, SHARE, HALF),
            buf(BF16, NZ - 1, SHARE, HALF),
            buf(BF16, SHARE, HALF),
            buf(BF16, SHARE, HALF),
            buf(BF16, NX - 1, SHARE, HALF),
            buf(BF16, NY, SHARE, HALF),
            dma(10), dma(NX - 1), dma(NX - 1), dma(2),
            dma(NZ - 1), dma(NZ - 1), dma(NY, NX), dma(NY, NX),
            dma(NZ - 1), dma(NZ - 1), dma(NX - 1), dma(NX - 1), dma(NX), dma(NX),
            dma(NY - 1, NX), dma(NY - 1, NX), dma(NX - 1, NX), dma(NX - 1, NX),
            dma(NX, 2), dma(NZ - 1), dma(NX, 2), dma(NZ - 1),
            dma(NX - 1), dma(NX - 1), dma(NX), dma(NY),
        ],
        compiler_params=pltpu.CompilerParams(
            collective_id=0, has_side_effects=True, vmem_limit_bytes=56 * 1024 * 1024
        ),
        cost_estimate=pl.CostEstimate(
            flops=11_000_000_000, bytes_accessed=8_000_000, transcendentals=4_000_000
        ),
    )(
        queries, features, class_weight, trunk_weight, targets, matches, head_rows,
        jnp.asarray(box_prior(ROWS)),
    )
    results = tuple(
        pltpu.with_memory_space_constraint(r, pltpu.VMEM) for r in (loss, query, classes, box, side)
    )
    loss, query, classes, box, side = pl.pallas_call(
        finish,
        out_shape=tuple(jax.ShapeDtypeStruct(r.shape, F32) for r in results),
        in_specs=[vmem] * 5,
        out_specs=[vmem] * 5,
    )(*results)
    return loss[0, 0], query, classes, box, side


def solution(mesh):
    in_specs = (
        P(("dp", "group"), None, None),
        P(("dp", "group"), None, None),
        P(("dp", "group"), None),
        P(("dp", "group"), None),
        P(),
        P(),
        P(),
    )
    out_specs = (P(), P(("dp", "group"), None), P("dp", None), P(), P())
    return jax.shard_map(
        on_device, mesh=mesh, in_specs=in_specs, out_specs=out_specs, check_vma=False
    )
```

```python
import functools

import jax
import jax.numpy as jnp
import numpy as np
from jax import lax
from jax.experimental import pallas as pl
from jax.experimental.pallas import tpu as pltpu
from jax.sharding import PartitionSpec as P

MESH = pl.DeviceIdType.MESH
F32 = jnp.float32
BF16 = jnp.bfloat16

GRID = 72
QUANT = 1024
ALPHA = 0.25
GIOU_WEIGHT = 2.0
LOGIT_BIAS = -4.0
EPSILON = 1e-06
LOG2E = 1.4426950408889634

NX, NY, NZ, NC = 4, 4, 8, 2
E, D, ROWS, Q = 1024, 768, 1536, 384
QROWS = Q // NX
SHARE = E // (NZ * NY * NC)
HALF = D // 2
BLOCK = 768
TILE = 256
CHUNKS = ((0, 256), (256, 512), (768, 768))
ORDER = (0, 1, 3, 2)
EARLY = 3
PEERS = 1 + (NX * NY - 1) + (NZ - 1)


def contract(left, right, left_dim, right_dim):
    return lax.dot_general(
        left, right, (((left_dim,), (right_dim,)), ((), ())), preferred_element_type=F32
    )


def box_prior(length):
    index = np.arange(length)

    def logit(value):
        return np.log(value) - np.log1p(-value)

    across = logit((index % GRID + 0.5) / GRID)
    down = logit((index // GRID + 0.5) / GRID)
    size = np.full((length,), logit(1.0 / GRID))
    return np.stack([across, down, size, size], 0).astype(np.float32)


def box_loss(box_raw, corners, weight):
    box = jax.nn.sigmoid(box_raw)
    cx, cy, bw, bh = (box[i : i + 1] for i in range(4))
    c0, c1, c2, c3 = (corners[i : i + 1] for i in range(4))
    left = cx - 0.5 * bw
    right = cx + 0.5 * bw
    top = cy - 0.5 * bh
    bottom = cy + 0.5 * bh
    inter_w = jnp.maximum(jnp.minimum(right, c2) - jnp.maximum(left, c0), 0.0)
    inter_h = jnp.maximum(jnp.minimum(bottom, c3) - jnp.maximum(top, c1), 0.0)
    inter = inter_w * inter_h
    union = bw * bh + (c2 - c0) * (c3 - c1) - inter
    outer_w = jnp.maximum(right, c2) - jnp.minimum(left, c0)
    outer_h = jnp.maximum(bottom, c3) - jnp.minimum(top, c1)
    enclose = outer_w * outer_h
    giou = inter / union - (enclose - union) / enclose
    return weight * (1.0 - giou)


def gelu(value):
    inner = value * (0.7978845608028654 + 0.035677408136300125 * (value * value))
    half = 0.5 * value
    return half + half * jnp.tanh(inner)


def rows_of(index, size):
    return pl.ds(pl.multiple_of(index * size, size), size)


def kernel(
    queries_hbm, features_hbm, cw_hbm, tw_hbm, targets_hbm, matches_hbm, heads_hbm, prior_hbm,
    loss_out, query_out, class_out, box_out, side_out,
    targets_ref, matches_ref, heads_ref, prior_ref, feat, cw, tw, own_q, all_q, unit_q, exact, inv_norm, units, hidden, raw, side,
    cosine, grads, sum_shift, sum_scale, d_rows, d_emb, small, small_p, small_two, small_z, small_v, small_xy, small_sum,
    small_all, q_send, q_recv, g_both, g_recv, s0, s1, r1y, r1x, t0, t1, r2a, r2b, u0, u1, r3a, r3b,
    load_sem, q_ssem, q_rsem, sp_sem, sz_ssem, sz_rsem, sxy_ssem, sxy_rsem,
    sa_ssem, sa_rsem, qs_ssem, qs_rsem, gp_ssem, gp_rsem, y1_ssem, y1_rsem, x1_ssem, x1_rsem,
    z0_ssem, z0_rsem, z1_ssem, z1_rsem, f0_ssem, f0_rsem, f1_ssem, f1_rsem,
):
    dp = lax.axis_index("dp")
    x = lax.axis_index("group")
    core = dp % NC
    y = (dp // NC) % NY
    z = dp // (NC * NY)

    def at(zz, yy, cc, xx):
        return ((zz * NY + yy) * NC + cc, xx)

    pair = at(z, y, 1 - core, x)
    x_peer = lambda d: at(z, y, core, (x + d) % NX)
    y_peer = lambda d: at(z, (y + d) % NY, core, x)
    xy_peer = lambda dy, dx: at(z, (y + dy) % NY, core, (x + dx) % NX)
    z_peer = lambda d: at((z + d) % NZ, y, core, x)
    xs, ys, zs = range(1, NX), range(1, NY), range(1, NZ)
    plane = [(dy, dx) for dy in range(NY) for dx in range(NX) if dy or dx]

    def remote(src, dst, ssem, rsem, device):
        return pltpu.make_async_remote_copy(
            src_ref=src, dst_ref=dst, send_sem=ssem, recv_sem=rsem,
            device_id=device, device_id_type=MESH,
        )

    loads = [
        pltpu.make_async_copy(source, target, load_sem.at[i])
        for i, (source, target) in enumerate(
            [(cw_hbm, cw)]
            + [
                (features_hbm.at[0, pl.ds(start, size)], feat.at[pl.ds(start, size)])
                for start, size in CHUNKS
            ]
            + [
                (queries_hbm, own_q),
                (heads_hbm, heads_ref),
                (tw_hbm, tw),
                (prior_hbm, prior_ref),
                (targets_hbm.at[0], targets_ref),
                (matches_hbm, matches_ref),
            ]
        )
    ]
    for load in loads[:4]:
        load.start()

    barrier = pltpu.get_barrier_semaphore()
    peers = [pair] + [xy_peer(dy, dx) for dy, dx in plane] + [z_peer(d) for d in zs]
    for peer in peers:
        pl.semaphore_signal(barrier, inc=1, device_id=peer, device_id_type=MESH)
    def embed(start, size):
        rows = pl.ds(start, size)
        emb = contract(feat[rows, :], cw[...], 1, 0)
        inv = lax.rsqrt(jnp.sum(emb * emb, axis=1, keepdims=True) + EPSILON)
        unit = emb * inv
        exact[rows, :] = unit
        units[rows, :] = unit.astype(BF16)
        inv_norm[rows, :] = inv

    loads[0].wait()
    loads[1].wait()
    for load in loads[4:]:
        load.start()
    embed(*CHUNKS[0])
    loads[2].wait()
    embed(*CHUNKS[1])

    loads[4].wait()
    all_q[0] = own_q[...]
    pl.semaphore_wait(barrier, PEERS)
    q_copies = {
        d: remote(own_q, all_q.at[ORDER.index(NX - d)], q_ssem.at[d - 1], q_rsem.at[d - 1], x_peer(d))
        for d in (1, 3, 2)
    }
    for copy in q_copies.values():
        copy.start()
    loads[3].wait()
    embed(*CHUNKS[2])
    for load in loads[5:]:
        load.wait()

    def box_hidden(i, carry):
        rows = rows_of(i, BLOCK)
        block = feat[rows, :]
        hid = gelu(contract(block, tw[...], 1, 0)).astype(BF16)
        hidden[rows, :] = hid
        raw[:, rows] = contract(hid, heads_ref[...], 1, 1).T
        side[:, rows] = contract(block, heads_ref[...], 1, 1).T
        return carry

    lax.fori_loop(0, ROWS // BLOCK, box_hidden, 0)

    matches = matches_ref[...]
    weight = (matches >= 0).astype(F32)
    corners = targets_ref[...].astype(F32) * (1.0 / QUANT)
    terms, pullback = jax.vjp(
        lambda value: box_loss(value, corners, weight), raw[0:4, :] + prior_ref[...]
    )
    d_raw = (GIOU_WEIGHT * pullback(jnp.ones_like(terms))[0]).astype(BF16)
    small[0:4, :] = contract(d_raw, hidden[...], 1, 0)

    def normalise(slot):
        rows = all_q[slot].astype(F32)
        inv = lax.rsqrt(jnp.sum(rows * rows, axis=1, keepdims=True) + EPSILON)
        unit_q[slot * QROWS : (slot + 1) * QROWS, :] = (rows * inv).astype(BF16)

    step = 32

    def focal(first, last, i, loss_sum):
        rows = slice(first * QROWS, last * QROWS)
        cosine[rows, :] = contract(unit_q[rows, :], units[rows_of(i, BLOCK), :], 1, 1)

        def tile(n, loss_sum):
            cols = rows_of(i * (BLOCK // TILE) + n, TILE)
            here = rows_of(n, TILE)
            shift = side[4:5, cols] + LOGIT_BIAS
            pre = side[5:6, cols]
            decay = jnp.exp(jnp.minimum(pre, 0.0))
            scale = jnp.where(pre > 0, pre + 1.0, decay)
            scale_two = scale * LOG2E
            match = matches_ref[:, cols]

            def block(j, target, carry):
                loss, d_shift, d_scale = carry
                rows = rows_of(j, step)
                base = cosine[rows, here] + shift
                hit = lax.broadcasted_iota(jnp.int32, (step, TILE), 0) == target
                logit = base * scale_two
                value = jnp.where(hit, -logit, logit)
                factor = jnp.where(hit, -ALPHA, 1.0 - ALPHA)
                power = jnp.exp2(jnp.minimum(value, 100.0))
                log_one = jnp.where(
                    power < 2.0**-8, power * (LOG2E - power * (LOG2E / 2 - power * (LOG2E / 3))), jnp.log2(1.0 + power)
                )
                neg_log = jnp.maximum(log_one, value)
                prob = jnp.exp2(value - neg_log)
                other = jnp.exp2(-neg_log)
                square = factor * (prob * prob)
                loss = loss + (jnp.abs(square) * neg_log).reshape(step // 8, 8, TILE).sum(0)
                d_logit = square * (prob + (2.0 / LOG2E) * (other * neg_log))
                d_shift = d_shift + d_logit.reshape(step // 8, 8, TILE).sum(0)
                d_scale = d_scale + (d_logit * base).reshape(step // 8, 8, TILE).sum(0)
                grads[rows, cols] = (d_logit * scale).astype(BF16)
                return loss, d_shift, d_scale

            def query_block(slot, carry):
                owner = (x + slot + slot // 2 - 2 * (slot // 3)) % NX
                target = match - owner * QROWS
                for part in range(QROWS // step):
                    carry = block(slot * (QROWS // step) + part, target - part * step, carry)
                return carry

            if first:
                d_shift, d_scale = sum_shift[:, cols], sum_scale[:, cols]
            else:
                d_shift = d_scale = jnp.zeros((8, TILE), F32)
            loss, d_shift, d_scale = lax.fori_loop(
                first, last, query_block, (loss_sum, d_shift, d_scale)
            )
            sum_shift[:, cols], sum_scale[:, cols] = d_shift, d_scale
            return loss

        return lax.fori_loop(0, BLOCK // TILE, tile, loss_sum)

    q_copies[1].wait_recv()
    q_copies[3].wait_recv()
    q_copies[2].wait_recv()
    for slot in range(4):
        normalise(slot)
    focal_sum = lax.fori_loop(
        0, ROWS // BLOCK, functools.partial(focal, 0, NX), jnp.zeros((8, TILE), F32)
    )

    def embedding_grad(i, carry):
        rows = rows_of(i, BLOCK)
        d_units = contract(grads[:, rows], unit_q[...], 0, 0)
        unit = exact[rows, :]
        along = jnp.sum(unit * d_units, axis=1, keepdims=True)
        d_emb[rows, :] = ((d_units - unit * along) * inv_norm[rows, :]).astype(BF16)
        return carry

    lax.fori_loop(0, ROWS // BLOCK, embedding_grad, 0)

    def pair_copy(k):
        return remote(g_both.at[1 - core, k], g_recv.at[k], gp_ssem.at[k], gp_rsem.at[k], pair)

    def y1_copy(k, d):
        return remote(s0.at[(y + d) % NY, k], r1y.at[d - 1, k], y1_ssem.at[d - 1, k], y1_rsem.at[d - 1, k], y_peer(d))

    def x1_copy(k, d):
        return remote(s1.at[(x + d) % NX, k], r1x.at[d - 1, k], x1_ssem.at[d - 1, k], x1_rsem.at[d - 1, k], x_peer(d))

    def z_copy(half, k, h):
        distance = (k + NX * h - z + NZ) % NZ
        slot = jnp.maximum(distance - 1, 0)
        source, target, ssem, rsem = ((t0, r2a, z0_ssem, z0_rsem), (t1, r2b, z1_ssem, z1_rsem))[half]
        return distance, remote(
            source.at[k, h], target.at[slot], ssem.at[k, h], rsem.at[slot], z_peer(distance)
        )

    def produce(k):
        left = jnp.concatenate(
            [feat[:, k * 128 : (k + 1) * 128], feat[:, (k + NX) * 128 : (k + NX + 1) * 128]], axis=1
        )
        for n in range(D // TILE):
            cols = slice(n * TILE, (n + 1) * TILE)
            part = contract(left, d_emb[:, cols], 0, 0).astype(BF16)
            part = part.reshape(2, NY, NC, SHARE, TILE)
            for cc in range(NC):
                g_both[cc, k, :, :, :, cols] = part[:, :, cc]
        pair_copy(k).start()

    def consume(k):
        pair_copy(k).wait_recv()
        for h in range(2):
            both = (g_both[core, k, h].astype(F32) + g_recv[k, h].astype(F32)).astype(BF16)
            for yy in range(NY):
                s0[yy, k, h] = both[yy, :, 0:HALF]
                s1[yy, k, h] = both[yy, :, HALF:D]
        for d in ys:
            y1_copy(k, d).start()
        for d in xs:
            x1_copy(k, d).start()

    def forward(k):
        for half in range(2):
            own, got, copy, mine = ((s0, r1y, y1_copy, y), (s1, r1x, x1_copy, x))[half]
            total = own[mine, k].astype(F32)
            for d in ys:
                copy(k, d).wait_recv()
                total = total + got[d - 1, k].astype(F32)
            (t0, t1)[half][k] = total.astype(BF16)
            for h in range(2):
                distance, move = z_copy(half, k, h)
                pl.when(distance != 0)(move.start)

    produce(0)
    produce(1)
    consume(0)
    produce(2)
    consume(1)
    produce(3)
    consume(2)

    pre = side[5:6, :]
    d_rows[0:1, :] = jnp.sum(sum_shift[...], axis=0, keepdims=True)
    d_rows[1:2, :] = jnp.sum(sum_scale[...], axis=0, keepdims=True) * jnp.where(
        pre > 0, 1.0, jnp.exp(jnp.minimum(pre, 0.0))
    )
    small[4:6, :] = contract(d_rows[...].astype(BF16), feat[...], 1, 0)
    fold = lambda row: row[:, 0:512] + row[:, 512:1024] + row[:, 1024:1536]
    focal_row = jnp.sum(focal_sum, axis=0, keepdims=True) * (1.0 / LOG2E)
    small[6:7, 0:512] = GIOU_WEIGHT * fold(terms)
    small[6:7, 0:TILE] += focal_row
    small[6:7, 512:1024] = fold(weight)
    small[7:8, :] = jnp.zeros((1, E), F32)
    small_pair = remote(small, small_p, sp_sem.at[0], sp_sem.at[1], pair)
    small_pair.start()

    consume(3)
    small_pair.wait()
    for k in range(NZ):
        lanes = slice(k * 128, (k + 1) * 128)
        small_two[k] = small[:, lanes] + small_p[:, lanes]
    sz_copies = [
        remote(small_two.at[(z + d) % NZ], small_z.at[d - 1], sz_ssem.at[d - 1], sz_rsem.at[d - 1], z_peer(d))
        for d in zs
    ]
    for copy in sz_copies:
        copy.start()
    for n in range(D // TILE):
        cols = slice(n * TILE, (n + 1) * TILE)
        part = contract(grads[...], units[:, cols], 1, 0).astype(BF16)
        for g in range(NX):
            q_send[g, :, cols] = part[g * QROWS : (g + 1) * QROWS, :]
    qs_copies = [
        remote(q_send.at[ORDER.index(d)], q_recv.at[d - 1], qs_ssem.at[d - 1], qs_rsem.at[d - 1], x_peer(d))
        for d in xs
    ]
    for copy in qs_copies:
        copy.start()

    for k in range(NX):
        forward(k)
    for copy in sz_copies:
        copy.wait_recv()
    small_v[...] = (
        ((small_two[z] + small_z[0]) + (small_z[1] + small_z[2]))
        + ((small_z[3] + small_z[4]) + (small_z[5] + small_z[6]))
    )
    sxy_copies = [
        remote(small_v, small_xy.at[dy, dx], sxy_ssem.at[dy, dx], sxy_rsem.at[dy, dx], xy_peer(dy, dx))
        for dy, dx in plane
    ]
    for copy in sxy_copies:
        copy.start()

    def over_z(total, got, half):
        for d in zs:
            remote(t0.at[0, 0], got.at[d - 1], z0_ssem.at[0, 0], (z0_rsem, z1_rsem)[half].at[d - 1], z_peer(d)).wait_recv()
            total = total + got[d - 1].astype(F32)
        return total.astype(BF16)

    u0[...] = over_z(t0[z % NX, z // NX].astype(F32), r2a, 0)
    f0_copies = [remote(u0, r3a.at[d - 1], f0_ssem.at[d - 1], f0_rsem.at[d - 1], x_peer(d)) for d in xs]
    for copy in f0_copies:
        copy.start()
    u1[...] = over_z(t1[z % NX, z // NX].astype(F32), r2b, 1)

    def f1_copy(target):
        return remote(u1, r3b.at[y], f1_ssem.at[target], f1_rsem.at[y], at(z, x, core, target))

    for target in range(NX):
        itself = jnp.logical_and(y == x, x == target)
        pl.when(jnp.logical_not(itself))(f1_copy(target).start)

    @pl.when(y == x)
    def _():
        r3b[y] = u1[...]

    for copy in sxy_copies:
        copy.wait_recv()
    small_xy[0, 0] = small_v[...]
    line = [
        (small_xy[dy, 0] + small_xy[dy, 2]) + (small_xy[dy, 1] + small_xy[dy, 3]) for dy in range(NY)
    ]
    small_sum[...] = (line[0] + line[2]) + (line[1] + line[3])
    small_all[z] = small_sum[...]
    sa_copies = [
        remote(small_sum, small_all.at[z], sa_ssem.at[d - 1], sa_rsem.at[d - 1], z_peer(d)) for d in zs
    ]
    for copy in sa_copies:
        copy.start()

    for copy in qs_copies:
        copy.wait_recv()
    sums = q_send[0].astype(F32)
    for d in xs:
        sums = sums + q_recv[d - 1].astype(F32)
    mine = own_q[...].astype(F32)
    inv = lax.rsqrt(jnp.sum(mine * mine, axis=1, keepdims=True) + EPSILON)
    mine = mine * inv
    along = jnp.sum(mine * sums, axis=1, keepdims=True)
    query_raw = (sums - mine * along) * inv

    for copy in sa_copies:
        copy.wait_recv()
    for k in range(NZ):
        small[:, k * 128 : (k + 1) * 128] = small_all[k]
    per = 1.0 / jnp.sum(small[6:7, 512:1024], axis=1, keepdims=True)
    box_out[...] = small[0:4, :] * per
    side_out[...] = small[4:6, :] * per
    loss_out[...] = jnp.sum(small[6:7, 0:512], axis=1, keepdims=True) * per
    query_out[...] = query_raw * per

    for copy in f0_copies:
        copy.wait_recv()
    total = (u0[...].astype(F32) + r3a[1].astype(F32)) + (r3a[0].astype(F32) + r3a[2].astype(F32))
    class_out[:, 0:HALF] = total * per
    for source in range(NY):
        itself = jnp.logical_and(y == x, y == source)
        arrived = remote(u1, r3b.at[source], f1_ssem.at[0], f1_rsem.at[source], at(z, source, core, y))
        pl.when(jnp.logical_not(itself))(arrived.wait_recv)
    total = r3b[0].astype(F32)
    for source in range(1, NY):
        total = total + r3b[source].astype(F32)
    class_out[:, HALF:D] = total * per

    for k in range(NX):
        pair_copy(k).wait_send()
        for d in ys:
            y1_copy(k, d).wait_send()
            x1_copy(k, d).wait_send()
        for half in range(2):
            for h in range(2):
                distance, move = z_copy(half, k, h)
                pl.when(distance != 0)(move.wait_send)
    for copy in list(q_copies.values()) + qs_copies + sz_copies + sxy_copies + sa_copies + f0_copies:
        copy.wait_send()
    for target in range(NX):
        itself = jnp.logical_and(y == x, x == target)
        pl.when(jnp.logical_not(itself))(f1_copy(target).wait_send)


def finish(*refs):
    count = len(refs) // 2
    for i in range(count):
        refs[count + i][...] = refs[i][...]


def on_device(features, targets, matches, queries, class_weight, trunk_weight, head_rows):
    hbm = pl.BlockSpec(memory_space=pl.ANY)
    vmem = pl.BlockSpec(memory_space=pltpu.VMEM)
    dma = lambda *shape: pltpu.SemaphoreType.DMA(shape)
    buf = lambda kind, *shape: pltpu.VMEM(shape, kind)
    loss, query, classes, box, side = pl.pallas_call(
        kernel,
        out_shape=(
            pltpu.VMEM((1, 1), F32),
            pltpu.VMEM((QROWS, D), F32),
            pltpu.VMEM((SHARE, D), F32),
            pltpu.VMEM((4, E), F32),
            pltpu.VMEM((2, E), F32),
        ),
        in_specs=[hbm] * 8,
        out_specs=[vmem] * 5,
        scratch_shapes=[
            buf(jnp.int32, 4, ROWS),
            buf(jnp.int32, 1, ROWS),
            buf(BF16, 6, E),
            buf(F32, 4, ROWS),
            buf(BF16, ROWS, E),
            buf(BF16, E, D),
            buf(BF16, E, E),
            buf(BF16, QROWS, D),
            buf(BF16, NX, QROWS, D),
            buf(BF16, Q, D),
            buf(F32, ROWS, D),
            buf(F32, ROWS, 1),
            buf(BF16, ROWS, D),
            buf(BF16, ROWS, E),
            buf(F32, 6, ROWS),
            buf(F32, 6, ROWS),
            buf(F32, Q, BLOCK),
            buf(BF16, Q, ROWS),
            buf(F32, 8, ROWS),
            buf(F32, 8, ROWS),
            buf(F32, 2, ROWS),
            buf(BF16, ROWS, D),
            buf(F32, 8, E),
            buf(F32, 8, E),
            buf(F32, NZ, 8, 128),
            buf(F32, NZ - 1, 8, 128),
            buf(F32, 8, 128),
            buf(F32, NY, NX, 8, 128),
            buf(F32, 8, 128),
            buf(F32, NZ, 8, 128),
            buf(BF16, NX, QROWS, D),
            buf(BF16, NX - 1, QROWS, D),
            buf(BF16, NC, NX, 2, NY, SHARE, D),
            buf(BF16, NX, 2, NY, SHARE, D),
            buf(BF16, NY, NX, 2, SHARE, HALF),
            buf(BF16, NY, NX, 2, SHARE, HALF),
            buf(BF16, NY - 1, NX, 2, SHARE, HALF),
            buf(BF16, NX - 1, NX, 2, SHARE, HALF),
            buf(BF16, NX, 2, SHARE, HALF),
            buf(BF16, NX, 2, SHARE, HALF),
            buf(BF16, NZ - 1, SHARE, HALF),
            buf(BF16, NZ - 1, SHARE, HALF),
            buf(BF16, SHARE, HALF),
            buf(BF16, SHARE, HALF),
            buf(BF16, NX - 1, SHARE, HALF),
            buf(BF16, NY, SHARE, HALF),
            dma(10), dma(NX - 1), dma(NX - 1), dma(2),
            dma(NZ - 1), dma(NZ - 1), dma(NY, NX), dma(NY, NX),
            dma(NZ - 1), dma(NZ - 1), dma(NX - 1), dma(NX - 1), dma(NX), dma(NX),
            dma(NY - 1, NX), dma(NY - 1, NX), dma(NX - 1, NX), dma(NX - 1, NX),
            dma(NX, 2), dma(NZ - 1), dma(NX, 2), dma(NZ - 1),
            dma(NX - 1), dma(NX - 1), dma(NX), dma(NY),
        ],
        compiler_params=pltpu.CompilerParams(
            collective_id=0, has_side_effects=True, vmem_limit_bytes=56 * 1024 * 1024
        ),
        cost_estimate=pl.CostEstimate(
            flops=11_000_000_000, bytes_accessed=8_000_000, transcendentals=4_000_000
        ),
    )(
        queries, features, class_weight, trunk_weight, targets, matches, head_rows,
        jnp.asarray(box_prior(ROWS)),
    )
    results = tuple(
        pltpu.with_memory_space_constraint(r, pltpu.VMEM) for r in (loss, query, classes, box, side)
    )
    loss, query, classes, box, side = pl.pallas_call(
        finish,
        out_shape=tuple(jax.ShapeDtypeStruct(r.shape, F32) for r in results),
        in_specs=[vmem] * 5,
        out_specs=[vmem] * 5,
    )(*results)
    return loss[0, 0], query, classes, box, side


def solution(mesh):
    in_specs = (
        P(("dp", "group"), None, None),
        P(("dp", "group"), None, None),
        P(("dp", "group"), None),
        P(("dp", "group"), None),
        P(),
        P(),
        P(),
    )
    out_specs = (P(), P(("dp", "group"), None), P("dp", None), P(), P())
    return jax.shard_map(
        on_device, mesh=mesh, in_specs=in_specs, out_specs=out_specs, check_vma=False
    )
```
